512 devices in a mesh: bl: 128 (over y, z, core), ch: 4 (over x).
Axes of the slice: x: 4, y: 4, z: 16, core: 2. Of those that a mesh axis runs over, the one named last changes fastest.
Arguments:
- sky_model_visibility: bfloat16 [2, 16384, 2048], P(None, 'bl', 'ch'), may hold values from -1 to 1
- measured_visibility: float32 [2, 16384, 64], P(None, 'bl', 'ch'), may hold values from -6 to 6
- rejected_cell_tally: int32 [16384, 64], P('bl', 'ch'), may hold values from 0 to 16
- station_pair_index: int32 [16384, 2], P('bl'), may hold values from 0 to 63, as said below
- fetch_lists: int32 [128, 64], replicated, may hold values from 0 to 511, as said below
- gain_values: float32 [2, 512, 2048], P(None, 'bl', 'ch'), may hold values from -5 to 5
- first_moment: float32 [2, 512, 2048], P(None, 'bl', 'ch'), may hold values from -0.3 to 0.3
- second_moment: float32 [2, 512, 2048], P(None, 'bl', 'ch'), may hold values from 0.004 to 0.02
Outputs:
- new_gains: float32 [2, 512, 2048], P(None, 'bl', 'ch')
- new_first: float32 [2, 512, 2048], P(None, 'bl', 'ch')
- new_second: float32 [2, 512, 2048], P(None, 'bl', 'ch')
- residual: float32 [2, 16384, 64], P(None, 'bl', 'ch')
The draws below stay inside these ranges and needn't reach their ends.
Inputs may be any that keep to these rules, and one draw needn't show every extreme that they name: `fetch_lists`: entries of one row are distinct stations; a row takes exactly 1 stations from each block of 4 consecutive stations that it touches. `station_pair_index`: in each block of 128 rows, every row holds two positions i < j, and no pair repeats within the block.
All inputs are finite; a program needn't handle non-finite values.
Results may differ from the reference program's by a relative error of at most 0.00035.
Values sent between devices are 32-bit elements; how exact they have to be, the bound alone decides.
A program may use at most 64 MiB of HBM per device.

```python
import math
import jax
import jax.numpy as jnp
import numpy as np
from jax import lax

SKY_SOURCES = 32
SPECTRAL_BINS = 64
ANTENNA_NUMBER = 512
ANTENNA_LINKS_PART = 128
NFETCH = 64
CELL_READINGS = 16
ITERS = 2
STEP = 3
ALL_ANTENNA_LINKS = 16384


def draw_fetch_lists(key, part):
    key = jax.random.fold_in(key, 11)
    segment_sequence = ALL_ANTENNA_LINKS // ANTENNA_LINKS_PART
    keep = ANTENNA_NUMBER // segment_sequence
    per_owner = max(1, NFETCH // segment_sequence)
    groups = NFETCH // per_owner

    def one_row(row_key):
        owner_key, local_key = jax.random.split(row_key)
        owners = jax.random.permutation(owner_key, segment_sequence)[:groups]
        locals_drawn = jax.vmap(lambda inner_key: jax.random.permutation(inner_key, keep)[:per_owner])(jax.random.split(local_key, groups))
        return (owners[:, None] * keep + locals_drawn).reshape(NFETCH)
    return jax.vmap(one_row)(jax.random.split(key, segment_sequence)).astype(jnp.int32)


def draw_station_pair_index(key, part):
    key = jax.random.fold_in(key, 23)
    first, second = np.triu_indices(NFETCH, 1)
    tally_number = first.shape[0]
    table = jnp.asarray(np.stack([first, second], 1), dtype=jnp.int32)

    def lone_segment(block_key):
        selection_seed, permutation_seed = jax.random.split(block_key)
        nested_body = jax.random.permutation(selection_seed, tally_number - 2)[:ANTENNA_LINKS_PART - 2].astype(jnp.int32) + 1
        selected_rows = jnp.concatenate([jnp.array([0, tally_number - 1], dtype=jnp.int32), nested_body])
        selected_rows = selected_rows[jax.random.permutation(permutation_seed, ANTENNA_LINKS_PART)]
        return table[selected_rows]
    segment_sequence = jax.vmap(lone_segment)(jax.random.split(key, ALL_ANTENNA_LINKS // ANTENNA_LINKS_PART))
    return segment_sequence.reshape(ALL_ANTENNA_LINKS, 2).astype(jnp.int32)


def with_ends(drawn, rng, smallest, largest):
    longest = drawn.shape.index(max(drawn.shape))
    spots = []
    for shift in (0, 1):
        where = [jax.random.randint(jax.random.fold_in(rng, axis), (), 0, length) for axis, length in enumerate(drawn.shape)]
        where[longest] = (where[longest] + shift) % drawn.shape[longest]
        spots.append(tuple(where))
    return drawn.at[spots[0]].set(smallest).at[spots[1]].set(largest)


def steps_of(stream_key, shape, shards, smallest, top_value):
    factor_of = 1.0
    for position, parts in shards:
        heights = jax.random.uniform(jax.random.fold_in(jax.random.fold_in(stream_key, 6), position), (parts,), jnp.float32, smallest / len(shards), top_value / len(shards))
        factor_of = factor_of * jnp.repeat(jnp.exp(heights), shape[position] // parts).reshape((-1,) + (1,) * (len(shape) - 1 - position))
    return factor_of


def centred(rng, extent, spread, reach, pieces=(), held_as=jnp.bfloat16):
    drawn = jax.random.normal(rng, extent, jnp.float32) * spread
    if len(pieces) > 0:
        drawn = steps_of(rng, extent, pieces, -0.22, 0.18) * drawn
    return jnp.clip(drawn, min=-reach, max=reach).astype(held_as)


def setup_inputs(seed: int = 0) -> dict:
    splits = jax.random.split(jax.random.key(seed), 9)
    return {
        "sky_model_visibility": centred(splits[0], (2, ALL_ANTENNA_LINKS, SPECTRAL_BINS * SKY_SOURCES), SKY_SOURCES ** -0.5, 1.0, ((1, 128), (2, 4))),
        "measured_visibility": centred(splits[1], (2, ALL_ANTENNA_LINKS, SPECTRAL_BINS), 1.0, 6.0, ((1, 128), (2, 4)), jnp.float32),
        "rejected_cell_tally": with_ends(jax.random.randint(splits[2], (ALL_ANTENNA_LINKS, SPECTRAL_BINS), 0, CELL_READINGS + 1), jax.random.fold_in(splits[2], 1), 0, CELL_READINGS).astype(jnp.int32),
        "station_pair_index": draw_station_pair_index(jax.random.fold_in(splits[8], 71), 0),
        "fetch_lists": draw_fetch_lists(jax.random.fold_in(splits[8], 71), 0),
        "gain_values": centred(splits[5], (2, ANTENNA_NUMBER, SPECTRAL_BINS * SKY_SOURCES), 0.7, 5.0, ((1, 128), (2, 4)), jnp.float32),
        "first_moment": centred(splits[6], (2, ANTENNA_NUMBER, SPECTRAL_BINS * SKY_SOURCES), 0.05, 0.3, ((1, 128), (2, 4)), jnp.float32),
        "second_moment": jnp.clip(jnp.exp(math.log(0.02) - 1.6094378 * jax.random.uniform(splits[7], (2, ANTENNA_NUMBER, SPECTRAL_BINS * SKY_SOURCES), jnp.float32) ** steps_of(splits[7], (2, ANTENNA_NUMBER, SPECTRAL_BINS * SKY_SOURCES), ((1, 128), (2, 4)), -0.2, 0.2)), 0.004, 0.02),
    }


BETA_ONE = 0.9
BETA_TWO = 0.99
ADAM_EPSILON = 1e-08
LEARN_RATE = 0.3
BLEND = 0.5
HIGHEST = lax.Precision.HIGHEST

def channel_kernel(nchan):
    chans = jnp.arange(nchan, dtype=jnp.float32)
    dist = jnp.abs(chans[:, None] - chans[None, :])
    raw = jnp.exp(-dist / (0.5 * nchan))
    return raw / lax.optimization_barrier(jnp.sum(raw, axis=1, keepdims=True))

def residual_terms(gain_first, gain_second, sky_model_visibility, measured_visibility, reliability_scale, spectral_blend_weight):
    a = gain_first[0]
    b = gain_first[1]
    c = gain_second[0]
    d = gain_second[1]
    coh_real = sky_model_visibility[0].astype(jnp.float32)
    coh_imag = sky_model_visibility[1].astype(jnp.float32)
    u = a * c + b * d
    v = b * c - a * d
    rows_here = a.shape[0]
    model_real = lax.optimization_barrier(jnp.sum((u * coh_real - v * coh_imag).reshape(rows_here, -1, SKY_SOURCES), axis=2))
    model_imag = lax.optimization_barrier(jnp.sum((u * coh_imag + v * coh_real).reshape(rows_here, -1, SKY_SOURCES), axis=2))
    err_real = reliability_scale * (measured_visibility[0] - model_real)
    err_imag = reliability_scale * (measured_visibility[1] - model_imag)
    wide = (rows_here, err_real.shape[1], SKY_SOURCES)
    spread_real = jnp.broadcast_to(err_real[:, :, None], wide).reshape(rows_here, -1)
    spread_imag = jnp.broadcast_to(err_imag[:, :, None], wide).reshape(rows_here, -1)
    x = c * coh_real + d * coh_imag
    y = d * coh_real - c * coh_imag
    grad_first = spectral_blend_weight * jnp.stack([spread_real * x - spread_imag * y, spread_real * y + spread_imag * x])
    x = a * coh_real - b * coh_imag
    y = a * coh_imag + b * coh_real
    grad_second = spectral_blend_weight * jnp.stack([spread_real * x + spread_imag * y, spread_real * y - spread_imag * x])
    return (jnp.stack([err_real, err_imag]), grad_first, grad_second)

def adam_update(current, moment_one, moment_two, smoothed, tally_number):
    moment_one = BETA_ONE * moment_one + (1.0 - BETA_ONE) * smoothed
    moment_two = BETA_TWO * moment_two + (1.0 - BETA_TWO) * smoothed * smoothed
    first_hat = moment_one / (1.0 - BETA_ONE ** tally_number)
    second_hat = moment_two / (1.0 - BETA_TWO ** tally_number)
    current = current - LEARN_RATE * first_hat / (jnp.sqrt(second_hat) + ADAM_EPSILON)
    return (current, moment_one, moment_two)

def gradient_pass(current, sky_model_visibility, measured_visibility, reliability_scale, left_antenna, right_antenna, spectral_blend_weight):

    def segment_member(position_number, carry):
        totals, residual = carry
        offset_begin = (position_number * ANTENNA_LINKS_PART).astype(jnp.int32)
        left_antenna_numbers = lax.dynamic_slice_in_dim(left_antenna, offset_begin, ANTENNA_LINKS_PART)
        right_antenna_numbers = lax.dynamic_slice_in_dim(right_antenna, offset_begin, ANTENNA_LINKS_PART)
        model_segment = lax.dynamic_slice_in_dim(sky_model_visibility, offset_begin, ANTENNA_LINKS_PART, 1)
        measured_segment = lax.dynamic_slice_in_dim(measured_visibility, offset_begin, ANTENNA_LINKS_PART, 1)
        reliability_segment = lax.dynamic_slice_in_dim(reliability_scale, offset_begin, ANTENNA_LINKS_PART, 0)
        gain_first = jnp.take(current, left_antenna_numbers, axis=1)
        gain_second = jnp.take(current, right_antenna_numbers, axis=1)
        part_res, grad_first, grad_second = residual_terms(gain_first, gain_second, model_segment, measured_segment, reliability_segment, spectral_blend_weight)
        totals = totals.at[:, left_antenna_numbers, :].add(grad_first).at[:, right_antenna_numbers, :].add(grad_second)
        residual = lax.dynamic_update_slice_in_dim(residual, part_res, offset_begin, 1)
        return (totals, residual)
    starting_state = (jnp.zeros(current.shape, current.dtype), jnp.zeros(measured_visibility.shape, measured_visibility.dtype))
    return lax.fori_loop(0, ALL_ANTENNA_LINKS // ANTENNA_LINKS_PART, segment_member, starting_state)

def reference(sky_model_visibility, measured_visibility, rejected_cell_tally, station_pair_index, fetch_lists, gain_values, first_moment, second_moment):
    owning_device_lookup = jnp.arange(ALL_ANTENNA_LINKS, dtype=jnp.int32) // ANTENNA_LINKS_PART
    left_antenna = fetch_lists[owning_device_lookup, station_pair_index[:, 0]].astype(jnp.int32)
    right_antenna = fetch_lists[owning_device_lookup, station_pair_index[:, 1]].astype(jnp.int32)
    reliability_scale = (CELL_READINGS - rejected_cell_tally).astype(jnp.float32) / CELL_READINGS
    spectral_blend_weight = -2.0 / math.sqrt(2.0 * ALL_ANTENNA_LINKS / ANTENNA_NUMBER)
    kernel = channel_kernel(SPECTRAL_BINS)
    current = gain_values
    moment_one = first_moment
    moment_two = second_moment
    residual = jnp.zeros(measured_visibility.shape, measured_visibility.dtype)
    for iteration in range(ITERS):
        totals, residual = gradient_pass(current, sky_model_visibility, measured_visibility, reliability_scale, left_antenna, right_antenna, spectral_blend_weight)
        grouped = totals.reshape(2, ANTENNA_NUMBER, SPECTRAL_BINS, SKY_SOURCES)
        blended = jnp.einsum('fg,csgk->csfk', kernel, grouped, precision=HIGHEST)
        smoothed = (1.0 - BLEND) * totals + BLEND * blended.reshape(totals.shape)
        current, moment_one, moment_two = adam_update(current, moment_one, moment_two, smoothed, STEP + iteration + 1)
    return (current, moment_one, moment_two, residual)
```

```python
import math

import jax
import jax.numpy as jnp
from jax import lax
from jax.experimental import pallas as pl
from jax.experimental.pallas import tpu as pltpu
from jax.sharding import PartitionSpec as P

MESH = pl.DeviceIdType.MESH
F32, BF16, I32 = jnp.float32, jnp.bfloat16, jnp.int32

SKY_SOURCES = 32
CELL_READINGS = 16
ITERS = 2
STEP = 3
BETA_ONE = 0.9
BETA_TWO = 0.99
ADAM_EPSILON = 1e-08
LEARN_RATE = 0.3
BLEND = 0.5

NX, NY, NZ, NS = 4, 4, 16, 8
NCHAN = 64
FAR = 5
CENTRES = (-FAR, 0, FAR)
STEPS = (1, -1, 2, -2)
ORDER = [j for j in CENTRES] + [j - n for n in STEPS for j in CENTRES] + [8]
SLOT = {rel % NZ: slot for slot, rel in enumerate(ORDER)}
NEAR_ROWS = 32 * len(CENTRES)
ROWS = 32 * NZ
PLANE = ((2, 0), (2, 1), (1, 0), (3, 0), (1, 1), (3, 1), (0, 1))
NBL = 128
CROWS = 136
DECAY = 2.0 / NCHAN


def remote(src, dst, send_sem, recv_sem, device):
    return pltpu.make_async_remote_copy(
        src_ref=src, dst_ref=dst, send_sem=send_sem, recv_sem=recv_sem, device_id=device, device_id_type=MESH
    )


def kernel(
    c_ref, meas_ref, rej_ref, pair_ref, fetch_ref, g_ref, m_ref, v_ref,
    go_ref, mo_ref, vo_ref, res_ref,
    csend, crecv, misc, pick, gsplit, grads, state_g, state_m, state_v,
    gpiece, zg, zp, rsn, rsh, accp, rsp, tots, xs, xr, ressend, resrecv, resmat,
    c_ss, c_rs, a1_ss, a1_rs, a2_ss, a2_rs, ah_ss, ah_rs, r1_ss, r1_rs, rh_ss, rh_rs, r2_ss, r2_rs, x_ss, x_rs, o_ss, o_rs,
):
    bl, x = lax.axis_index("bl"), lax.axis_index("ch")
    y, z, c = lax.div(bl, 2 * NZ), lax.rem(lax.div(bl, 2), NZ), lax.rem(bl, 2)
    s = 2 * y + c

    def device(s_to, dz=0, dx=0):
        z_to, x_to = lax.rem(z + dz + NZ, NZ), lax.rem(x + dx, NX)
        return ((lax.div(s_to, 2) * NZ + z_to) * 2 + lax.rem(s_to, 2), x_to)

    def mate(dy, dc):
        return 2 * lax.rem(y + dy, NY) + lax.rem(c + dc, 2)

    mates = [mate(dy, dc) for dy, dc in PLANE]

    barrier = pltpu.get_barrier_semaphore()
    partners = [device(s, j) if k == NS - 1 else device(mates[k], j) for j in CENTRES for k in range(NS) if j or k < NS - 1]
    partners += [device(s, n) for n in (1, -1, 2, -2, 3, -3)] + [device(s, 0, dx) for dx in (1, 2, 3)]
    for partner in partners:
        pl.semaphore_signal(barrier, inc=1, device_id=partner, device_id_type=MESH)

    lane8 = lax.broadcasted_iota(I32, (8, 128), 1)
    low8 = lane8 < 64

    def to_pieces(ref, out):
        for t in range(4):
            both = jnp.concatenate([ref[0, :, 128 * t : 128 * t + 128], ref[1, :, 128 * t : 128 * t + 128]], axis=0)
            turned = pltpu.roll(both, 64, 1)
            left = jnp.concatenate([both[0:4], turned[0:4]], axis=0)
            right = jnp.concatenate([turned[4:8], both[4:8]], axis=0)
            out[8 * t : 8 * t + 8, :] = jnp.where(low8, left, right)

    def from_pieces(value, ref):
        for t in range(4):
            both = value[8 * t : 8 * t + 8]
            turned = pltpu.roll(both, 64, 1)
            left = jnp.concatenate([both[0:4], turned[0:4]], axis=0)
            right = jnp.concatenate([turned[4:8], both[4:8]], axis=0)
            mixed = jnp.where(low8, left, right)
            ref[0, :, 128 * t : 128 * t + 128] = mixed[0:4]
            ref[1, :, 128 * t : 128 * t + 128] = mixed[4:8]

    to_pieces(g_ref, state_g)
    for k in range(NS):
        gpiece[0, k] = state_g[4 * k : 4 * k + 4, :]

    misc[:, 0:16] = meas_ref[0]
    misc[:, 16:32] = meas_ref[1]
    misc[:, 32:48] = (CELL_READINGS - rej_ref[...]).astype(F32) / CELL_READINGS
    fetch_row = fetch_ref[pl.ds(bl, 1), :].astype(F32)
    places = lax.broadcasted_iota(I32, (NBL, fetch_ref.shape[1]), 1)
    for i in range(2):
        station = jnp.where(pair_ref[:, i : i + 1] == places, fetch_row, 0.0)
        misc[:, 48 + i : 49 + i] = jnp.sum(station, axis=1, keepdims=True)
    turned = misc[...].T
    station = turned[48:50].astype(I32)
    rel = ((station >> 3) & (NZ - 1)) - z
    rel = jnp.where(rel < 0, rel + NZ, rel)
    slot = jnp.zeros_like(rel)
    for k in range(NZ):
        slot = jnp.where(rel == k, SLOT[k], slot)
    rows = (slot * 32 + (station >> 7) * 8 + (station & 7)).astype(F32)
    for t in range(4):
        for ri in range(2):
            block = c_ref[ri, :, 128 * t : 128 * t + 128].astype(F32).T
            csend[2 * t, 64 * ri : 64 * ri + 64] = block[0:64]
            csend[2 * t + 1, 64 * ri : 64 * ri + 64] = block[64:128]
    for k in range(NS):
        for i in range(3):
            csend[k, 128 + 2 * i : 130 + 2 * i] = turned[16 * i + 2 * k : 16 * i + 2 * k + 2]
        csend[k, 134:136] = rows

    pl.semaphore_wait(barrier, len(partners))

    def gains_copy(it, j, k):
        to = s if k is None else mates[k]
        return remote(
            gpiece.at[it, to], zg.at[it, 2 - j, s], a1_ss.at[it, j, to], a1_rs.at[it, 2 - j, s], device(to, CENTRES[j])
        )

    def gains_out(it):
        sent = []
        for j in (0, 2, 1):
            for k in [*range(NS - 1)] + ([None] if j != 1 else []):
                copy = gains_copy(it, j, k)
                copy.start()
                sent.append(copy)
        return sent

    def gains_on(it):
        sent = []
        zg[it, 1, s] = gpiece[it, s]
        for j in (1, 0, 2):
            for k in [*range(NS - 1)] + ([None] if j != 1 else []):
                source = s if k is None else mates[k]
                remote(
                    gpiece.at[it, s], zg.at[it, j, source], a1_ss.at[it, j, s], a1_rs.at[it, j, source], device(mates[0])
                ).wait_recv()
            for i, n in enumerate(STEPS):
                slot = 3 * (i + 1) + j
                copy = remote(zg.at[it, j], zg.at[it, slot], a2_ss.at[it, i, j], a2_rs.at[it, i, j], device(s, n))
                copy.start()
                sent.append(copy)
            if j != 1:
                half = pl.ds(2 * j, 4)
                copy = remote(
                    zg.at[it, j, half], zg.at[it, 15, half], ah_ss.at[it, j], ah_rs.at[it, j], device(s, 3 if j == 0 else -3)
                )
                copy.start()
                sent.append(copy)
        return sent

    def drain(copies):
        for copy in copies:
            copy.wait_send()

    sent_gains = gains_out(0)
    sent_c = []
    for k in range(NS - 1):
        copy = remote(csend.at[mates[k]], crecv.at[s], c_ss.at[mates[k]], c_rs.at[s], device(mates[k]))
        copy.start()
        sent_c.append(copy)
    crecv[s] = csend[s]
    to_pieces(m_ref, state_m)
    to_pieces(v_ref, state_v)
    sent_on = gains_on(0)

    def source_of(i):
        half = lax.div(i, 2)
        dy = jnp.where(half == 2, 3, jnp.where(half == 3, 2, half))
        return 2 * lax.rem(y + dy, NY) + lax.rem(c + i, 2)

    row_id = lax.broadcasted_iota(I32, (ROWS, NBL), 0)

    def picks(i, source):
        for k in range(2):
            row = crecv[source, 134 + k : 135 + k, :].astype(I32)
            where = pl.multiple_of(256 * i + 128 * k, 128)
            pick[:, pl.ds(where, 128)] = jnp.where(row_id == row, 1.0, 0.0).astype(BF16)

    picks(0, s)

    def next_picks(i, carry):
        source = source_of(i)
        remote(csend.at[0], crecv.at[source], c_ss.at[s], c_rs.at[source], device(mates[0])).wait_recv()
        picks(i, source)
        return carry

    lax.fori_loop(1, NS, next_picks, 0)

    lane32 = lax.broadcasted_iota(I32, (32, 128), 1)
    odd32 = (lane32 & 32) != 0
    odd8 = (lane8 & 32) != 0
    pair32 = lax.broadcasted_iota(I32, (32, 128), 0) >> 2
    chan = 2 * pair32 + jnp.where(odd32, 1, 0)
    a1 = math.exp(-DECAY)

    def decay(steps):
        return jnp.exp(-DECAY * steps.astype(F32))

    whole_chan = chan + 16 * x
    geometric = 1.0 / (1.0 - a1)
    norm = (1.0 - decay(whole_chan + 1)) * geometric + (a1 - decay(NCHAN - whole_chan)) * geometric
    half_norm = BLEND / norm
    from_left = decay(chan + 1)
    from_right = decay(16 - chan)
    near_left = jnp.where(odd32, a1 * a1, a1)
    near_right = jnp.where(odd32, a1, a1 * a1)
    up = jnp.where(odd32, 1.0, a1)
    down = jnp.where(odd32, a1, 1.0)

    def swap(value):
        return jnp.where((lax.broadcasted_iota(I32, value.shape, 1) & 32) != 0, pltpu.roll(value, 32, 1), pltpu.roll(value, 96, 1))

    def smooth(it):
        total = tots[...]
        swapped = swap(total)
        right_going = total * up + swapped * down
        left_going = total * down + swapped * up
        blended = total + a1 * swapped
        zero = jnp.zeros((4, 128), F32)
        lefts, rights = [zero], [zero]
        for k in range(NS):
            lefts.append(a1 * a1 * lefts[-1] + right_going[4 * k : 4 * k + 4])
            q = NS - 1 - k
            rights.append(a1 * a1 * rights[-1] + left_going[4 * q : 4 * q + 4])
        out8 = jnp.concatenate([jnp.where(odd8[0:4], rights[NS], lefts[NS])] * 2, axis=0)
        xs[it] = out8[0:4]
        sent = []
        for dx in (2, 1, 3):
            copy = remote(xs.at[it], xr.at[it, dx - 1], x_ss.at[it, dx - 1], x_rs.at[it, dx - 1], device(s, 0, dx))
            copy.start()
            sent.append(copy)
        left_all = jnp.concatenate(lefts[:NS], axis=0)
        right_all = jnp.concatenate(rights[NS - 1 :: -1], axis=0)
        blended = blended + near_left * left_all + near_right * right_all
        across = jnp.zeros((4, 128), F32)
        weights = []
        for dx in (1, 2, 3):
            source = lax.rem(x - dx + NX, NX)
            gap = jnp.full((8, 128), jnp.abs(x - source), I32)
            is_left = jnp.full((8, 128), x - source, I32) > 0
            used = jnp.where(is_left, jnp.where(odd8, 0, 1), jnp.where(odd8, 1, 0)).astype(F32)
            weights.append((used * decay(16 * (gap - 1)))[0:4])
        for dx in (1, 2, 3):
            remote(xs.at[it], xr.at[it, dx - 1], x_ss.at[it, dx - 1], x_rs.at[it, dx - 1], device(s, 0, dx)).wait_recv()
        for dx in (1, 2, 3):
            across = across + xr[it, dx - 1] * weights[dx - 1]
        across = jnp.concatenate([across] * 8, axis=0)
        other = swap(across)
        blended = blended + from_left * jnp.where(odd32, other, across) + from_right * jnp.where(odd32, across, other)
        return (1.0 - BLEND) * total + half_norm * blended, sent

    coef = -2.0 / math.sqrt(2.0 * NBL * NS * NZ / (4 * NS * NZ))

    for it in range(ITERS):
        last = it == ITERS - 1
        for j in (0, 1, 2):
            for i in range(len(STEPS)):
                slot = 3 * (i + 1) + j
                remote(
                    zg.at[it, j], zg.at[it, slot], a2_ss.at[it, i, j], a2_rs.at[it, i, j], device(s, STEPS[i])
                ).wait_recv()
        for j in (0, 2):
            half = pl.ds(2 * j, 4)
            remote(zg.at[it, j, half], zg.at[it, 15, half], ah_ss.at[it, j], ah_rs.at[it, j], device(s, 3)).wait_recv()
        for t in range(4):
            block = zg[it, 4 * t : 4 * t + 4].reshape(128, 128).T
            high = block.astype(BF16)
            gsplit[0:128, 128 * t : 128 * t + 128] = high
            gsplit[128:256, 128 * t : 128 * t + 128] = (block - high.astype(F32)).astype(BF16)

        def chunk(i, carry, last=last):
            source = source_of(i)
            at = pl.multiple_of(256 * i, 256)
            both = jnp.dot(gsplit[...], pick[:, pl.ds(at, 256)], preferred_element_type=F32)
            both = both[0:128] + both[128:256]
            ga, gb = both[0:64, 0:128], both[64:128, 0:128]
            gc, gd = both[0:64, 128:256], both[64:128, 128:256]
            cr, ci = crecv[source, 0:64, :], crecv[source, 64:128, :]
            u = ga * gc + gb * gd
            v = gb * gc - ga * gd
            model_re = jnp.sum((u * cr - v * ci).reshape(2, SKY_SOURCES, NBL), axis=1)
            model_im = jnp.sum((u * ci + v * cr).reshape(2, SKY_SOURCES, NBL), axis=1)
            weight = crecv[source, 132:134, :]
            err_re = weight * (crecv[source, 128:130, :] - model_re)
            err_im = weight * (crecv[source, 130:132, :] - model_im)
            if last:
                ressend[source] = jnp.concatenate([err_re, err_im], axis=0)
            wide = (2, SKY_SOURCES, NBL)
            sr = jnp.broadcast_to((coef * err_re)[:, None, :], wide).reshape(64, NBL)
            si = jnp.broadcast_to((coef * err_im)[:, None, :], wide).reshape(64, NBL)
            px = gc * cr + gd * ci
            py = gd * cr - gc * ci
            qx = ga * cr - gb * ci
            qy = ga * ci + gb * cr
            terms = ((sr * px - si * py, sr * py + si * px), (sr * qx + si * qy, sr * qy - si * qx))
            for k in range(2):
                for ri in range(2):
                    value = terms[k][ri]
                    high = value.astype(BF16)
                    where = pl.ds(pl.multiple_of(256 * i + 128 * k, 128), 128)
                    grads[64 * ri : 64 * ri + 64, where] = high
                    grads[128 + 64 * ri : 192 + 64 * ri, where] = (value - high.astype(F32)).astype(BF16)
            return carry

        lax.fori_loop(0, NS, chunk, 0)

        both = lax.dot_general(pick[...], grads[...], (((1,), (1,)), ((), ())), preferred_element_type=F32)
        zp[it] = both[:, 0:128] + both[:, 128:256]
        sent_near = []
        for i, n in enumerate(STEPS):
            copy = remote(
                zp.at[it, pl.ds(NEAR_ROWS * (i + 1), NEAR_ROWS)], rsn.at[it, i], r1_ss.at[it, i], r1_rs.at[it, i], device(s, -n)
            )
            copy.start()
            sent_near.append(copy)
        for h in range(2):
            copy = remote(
                zp.at[it, pl.ds(480 + 16 * h, 16)], rsh.at[it, h], rh_ss.at[it, h], rh_rs.at[it, h], device(s, 6 * h - 3)
            )
            copy.start()
            sent_near.append(copy)
        sent_res = []
        if last:
            for k in range(NS - 1):
                copy = remote(ressend.at[mates[k]], resrecv.at[s], o_ss.at[mates[k]], o_rs.at[s], device(mates[k]))
                copy.start()
                sent_res.append(copy)
            resrecv[s] = ressend[s]
        else:
            drain(sent_c)
        drain(sent_gains)
        drain(sent_on)
        for copy in sent_near:
            copy.wait_recv()
        acc = zp[it, 0:NEAR_ROWS, :]
        for i in range(len(STEPS)):
            acc = acc + rsn[it, i]
        parts = [acc[0:16] + rsh[it, 0], acc[16:32], acc[32:64], acc[64:80], acc[80:96] + rsh[it, 1]]
        acc = jnp.concatenate(parts, axis=0)
        for j in range(3):
            for k in range(NS):
                accp[it, j, k] = acc[32 * j + 4 * k : 32 * j + 4 * k + 4]
        sent_far = []
        for j in (0, 2, 1):
            for k in [*range(NS - 1)] + ([None] if j != 1 else []):
                to = s if k is None else mates[k]
                copy = remote(
                    accp.at[it, j, to], rsp.at[it, j, s], r2_ss.at[it, j, to], r2_rs.at[it, j, s], device(to, CENTRES[j])
                )
                copy.start()
                sent_far.append(copy)
        rsp[it, 1, s] = accp[it, 1, s]
        drain(sent_near)
        if last:
            drain(sent_res)
            for k in range(NS - 1):
                remote(
                    ressend.at[s], resrecv.at[mates[k]], o_ss.at[s], o_rs.at[mates[k]], device(mates[k])
                ).wait_recv()
            for k in range(NS):
                for ri in range(2):
                    resmat[16 * ri + 2 * k : 16 * ri + 2 * k + 2, :] = resrecv[k, 2 * ri : 2 * ri + 2, :]
            final = resmat[...].T
            res_ref[0] = final[:, 0:16]
            res_ref[1] = final[:, 16:32]
        for j in (1, 0, 2):
            for k in [*range(NS - 1)] + ([None] if j != 1 else []):
                source = s if k is None else mates[k]
                remote(
                    accp.at[it, j, s], rsp.at[it, j, source], r2_ss.at[it, j, s], r2_rs.at[it, j, source], device(mates[0])
                ).wait_recv()
        for k in range(NS):
            tots[4 * k : 4 * k + 4, :] = rsp[it, 0, k] + rsp[it, 1, k] + rsp[it, 2, k]

        smoothed, sent_x = smooth(it)
        tally = STEP + it + 1
        new_m = BETA_ONE * state_m[...] + (1.0 - BETA_ONE) * smoothed
        new_v = BETA_TWO * state_v[...] + (1.0 - BETA_TWO) * smoothed * smoothed
        first_hat = new_m / (1.0 - BETA_ONE**tally)
        second_hat = new_v / (1.0 - BETA_TWO**tally)
        new_g = state_g[...] - LEARN_RATE * first_hat / (jnp.sqrt(second_hat) + ADAM_EPSILON)
        if last:
            from_pieces(new_g, go_ref)
            from_pieces(new_m, mo_ref)
            from_pieces(new_v, vo_ref)
            drain(sent_far)
            drain(sent_x)
        else:
            for k in range(NS):
                gpiece[it + 1, k] = new_g[4 * k : 4 * k + 4]
            sent_gains = gains_out(it + 1)
            state_g[...] = new_g
            state_m[...] = new_m
            state_v[...] = new_v
            drain(sent_far)
            drain(sent_x)
            sent_on = gains_on(it + 1)


def on_device(*args):
    coherency, measured = args[0], args[1]
    gains = args[5]
    out = [jax.ShapeDtypeStruct(gains.shape, F32)] * 3 + [jax.ShapeDtypeStruct(measured.shape, F32)]
    vmem = pl.BlockSpec(memory_space=pltpu.VMEM)
    sem = pltpu.SemaphoreType.DMA
    buf = pltpu.VMEM
    return pl.pallas_call(
        kernel,
        out_shape=out,
        in_specs=[vmem] * 8,
        out_specs=[vmem] * 4,
        scratch_shapes=[
            buf((NS, CROWS, NBL), F32),
            buf((NS, CROWS, NBL), F32),
            buf((NBL, 128), F32),
            buf((ROWS, 2 * NBL * NS), BF16),
            buf((256, ROWS), BF16),
            buf((256, 2 * NBL * NS), BF16),
            buf((32, 128), F32),
            buf((32, 128), F32),
            buf((32, 128), F32),
            buf((ITERS, NS, 4, 128), F32),
            buf((ITERS, NZ, NS, 4, 128), F32),
            buf((ITERS, ROWS, 128), F32),
            buf((ITERS, 4, NEAR_ROWS, 128), F32),
            buf((ITERS, 2, 16, 128), F32),
            buf((ITERS, 3, NS, 4, 128), F32),
            buf((ITERS, 3, NS, 4, 128), F32),
            buf((32, 128), F32),
            buf((ITERS, 4, 128), F32),
            buf((ITERS, 3, 4, 128), F32),
            buf((NS, 4, 128), F32),
            buf((NS, 4, 128), F32),
            buf((128, 128), F32),
            sem((NS,)), sem((NS,)),
            sem((ITERS, 3, NS)), sem((ITERS, 3, NS)),
            sem((ITERS, 4, 3)), sem((ITERS, 4, 3)),
            sem((ITERS, 3)), sem((ITERS, 3)),
            sem((ITERS, 4)), sem((ITERS, 4)),
            sem((ITERS, 2)), sem((ITERS, 2)),
            sem((ITERS, 3, NS)), sem((ITERS, 3, NS)),
            sem((ITERS, 3)), sem((ITERS, 3)),
            sem((NS,)), sem((NS,)),
        ],
        compiler_params=pltpu.CompilerParams(collective_id=0, has_side_effects=True, vmem_limit_bytes=40 * 2**20),
        cost_estimate=pl.CostEstimate(flops=4 * 10**9, bytes_accessed=2**20, transcendentals=10**4),
        name="calibrate",
    )(*args)


def solution(mesh):
    split = P(None, "bl", "ch")
    return jax.shard_map(
        on_device,
        mesh=mesh,
        in_specs=(split, split, P("bl", "ch"), P("bl", None), P(), split, split, split),
        out_specs=(split,) * 4,
        check_vma=False,
    )
```

```python
import math

import jax
import jax.numpy as jnp
from jax import lax
from jax.experimental import pallas as pl
from jax.experimental.pallas import tpu as pltpu
from jax.sharding import PartitionSpec as P

MESH = pl.DeviceIdType.MESH
F32, BF16, I32 = jnp.float32, jnp.bfloat16, jnp.int32

SKY_SOURCES = 32
CELL_READINGS = 16
ITERS = 2
STEP = 3
BETA_ONE = 0.9
BETA_TWO = 0.99
ADAM_EPSILON = 1e-08
LEARN_RATE = 0.3
BLEND = 0.5

NX, NY, NZ, NS = 4, 4, 16, 8
NCHAN = 64
FAR = 5
CENTRES = (-FAR, FAR, 0)
STEPS = (1, -1, 2, -2)
ORDER = [-FAR, FAR] + [j - n for n in STEPS for j in (-FAR, FAR)] + [8] + [0] + [-n for n in STEPS]
SLOT = {rel % NZ: slot for slot, rel in enumerate(ORDER)}
OPPOSITE, OWN = 10, 11
HOME = (0, 1, OWN)
BACK = (1, 0, OWN)
ROWS = 32 * NZ
PLANE = ((2, 0), (2, 1), (1, 0), (3, 0), (1, 1), (3, 1), (0, 1))
NBL = 128
CROWS = 136
DECAY = 2.0 / NCHAN


def remote(src, dst, send_sem, recv_sem, device):
    return pltpu.make_async_remote_copy(
        src_ref=src, dst_ref=dst, send_sem=send_sem, recv_sem=recv_sem, device_id=device, device_id_type=MESH
    )


def kernel(
    c_hbm, meas_hbm, rej_hbm, pair_hbm, fetch_hbm, g_hbm, m_hbm, v_hbm,
    go_ref, mo_ref, vo_ref, res_ref,
    c_ref, meas_ref, rej_ref, pair_ref, fetch_ref, g_ref, m_ref, v_ref, in_sem,
    csend, crecv, pick, gsplit, grads, state_g, state_m, state_v,
    gpiece, zg, zp, rsn, rsc, rsh, accp, rsp, tots, xs, xr, ressend, resrecv,
    c_ss, c_rs, a1_ss, a1_rs, a2_ss, a2_rs, r1_ss, r1_rs, rc_ss, rc_rs, rh_ss, rh_rs, r2_ss, r2_rs, x_ss, x_rs, o_ss, o_rs,
):
    bl, x = lax.axis_index("bl"), lax.axis_index("ch")
    y, z, c = lax.div(bl, 2 * NZ), lax.rem(lax.div(bl, 2), NZ), lax.rem(bl, 2)
    s = 2 * y + c

    def device(s_to, dz=0, dx=0):
        z_to, x_to = lax.rem(z + dz + NZ, NZ), lax.rem(x + dx, NX)
        return ((lax.div(s_to, 2) * NZ + z_to) * 2 + lax.rem(s_to, 2), x_to)

    def mate(dy, dc):
        return 2 * lax.rem(y + dy, NY) + lax.rem(c + dc, 2)

    mates = [mate(dy, dc) for dy, dc in PLANE]

    barrier = pltpu.get_barrier_semaphore()
    partners = [device(s, j) if k == NS - 1 else device(mates[k], j) for j in CENTRES for k in range(NS) if j or k < NS - 1]
    partners += [device(s, n) for n in (1, -1, 2, -2, 3, -3)] + [device(s, 0, dx) for dx in (1, 2, 3)]
    for partner in partners:
        pl.semaphore_signal(barrier, inc=1, device_id=partner, device_id_type=MESH)

    loads = [
        pltpu.make_async_copy(src, dst, in_sem.at[i])
        for i, (src, dst) in enumerate(
            [
                (g_hbm, g_ref), (pair_hbm, pair_ref), (fetch_hbm, fetch_ref), (rej_hbm, rej_ref), (meas_hbm, meas_ref),
                (c_hbm, c_ref), (m_hbm, m_ref), (v_hbm, v_ref),
            ]
        )
    ]
    for load in loads:
        load.start()
    lane8 = lax.broadcasted_iota(I32, (8, 128), 1)
    low8 = lane8 < 64

    def to_pieces(ref, out):
        for t in range(4):
            both = jnp.concatenate([ref[0, :, 128 * t : 128 * t + 128], ref[1, :, 128 * t : 128 * t + 128]], axis=0)
            turned = pltpu.roll(both, 64, 1)
            left = jnp.concatenate([both[0:4], turned[0:4]], axis=0)
            right = jnp.concatenate([turned[4:8], both[4:8]], axis=0)
            out[8 * t : 8 * t + 8, :] = jnp.where(low8, left, right)

    def from_pieces(value, ref):
        for t in range(4):
            both = value[8 * t : 8 * t + 8]
            turned = pltpu.roll(both, 64, 1)
            left = jnp.concatenate([both[0:4], turned[0:4]], axis=0)
            right = jnp.concatenate([turned[4:8], both[4:8]], axis=0)
            mixed = jnp.where(low8, left, right)
            ref[0, :, 128 * t : 128 * t + 128] = mixed[0:4]
            ref[1, :, 128 * t : 128 * t + 128] = mixed[4:8]

    loads[0].wait()
    to_pieces(g_ref, state_g)
    for k in range(NS):
        gpiece[0, k] = state_g[4 * k : 4 * k + 4, :]

    for load in loads[1:5]:
        load.wait()
    fetch = jnp.where(lax.broadcasted_iota(I32, fetch_ref.shape, 1) == bl, fetch_ref[...], 0).astype(F32)
    fetch = jnp.sum(fetch, axis=1, keepdims=True)
    places = lax.broadcasted_iota(I32, (fetch_ref.shape[0], NBL), 0)
    station = jnp.concatenate(
        [
            jnp.sum(jnp.where(places == pair_ref[i : i + 1, :], fetch, 0.0), axis=0, keepdims=True)
            for i in range(2)
        ],
        axis=0,
    ).astype(I32)
    rel = ((station >> 3) & (NZ - 1)) - z
    rel = jnp.where(rel < 0, rel + NZ, rel)
    slot = jnp.zeros_like(rel)
    for k in range(NZ):
        slot = jnp.where(rel == k, SLOT[k], slot)
    weights = (CELL_READINGS - rej_ref[...]).astype(F32) / CELL_READINGS
    rows = (slot * 32 + (station >> 7) * 8 + (station & 7)).astype(F32)
    loads[5].wait()
    for t in range(4):
        for ri in range(2):
            block = c_ref[ri, :, 128 * t : 128 * t + 128].astype(F32).T
            csend[2 * t, 64 * ri : 64 * ri + 64] = block[0:64]
            csend[2 * t + 1, 64 * ri : 64 * ri + 64] = block[64:128]
    for k in range(NS):
        for ri in range(2):
            csend[k, 128 + 2 * ri : 130 + 2 * ri] = meas_ref[ri, 2 * k : 2 * k + 2, :]
        csend[k, 132:134] = weights[2 * k : 2 * k + 2]
        csend[k, 134:136] = rows

    pl.semaphore_wait(barrier, len(partners))

    def waiter(ref, send_sem, recv_sem):
        return remote(ref, ref, send_sem, recv_sem, device(mates[0]))

    def gains_out(it):
        for j in range(3):
            for k in [*range(NS - 1)] + ([None] if j != 2 else []):
                to = s if k is None else mates[k]
                remote(
                    gpiece.at[it, to], zg.at[it, BACK[j], s], a1_ss.at[it], a1_rs.at[it, (1, 0, 2)[j]], device(to, CENTRES[j])
                ).start()

    def gains_on(it):
        def near_copy(i, own):
            width = 1 if own else 2
            src, dst = (OWN, OWN + 1 + i) if own else (0, 2 + 2 * i)
            return remote(
                zg.at[it, pl.ds(src, width)], zg.at[it, pl.ds(dst, width)], a2_ss.at[it], a2_rs.at[it, own], device(s, STEPS[i])
            )

        def half_copy(h):
            half = pl.ds(4 * h, 4)
            return remote(
                zg.at[it, h, half], zg.at[it, OPPOSITE, half], a2_ss.at[it], a2_rs.at[it, 0], device(s, 3 - 6 * h)
            )

        zg[it, OWN, s] = gpiece[it, s]
        waiter(zg.at[it, OWN, pl.ds(0, NS - 1)], a1_ss.at[it], a1_rs.at[it, 2]).wait_recv()
        for i in range(len(STEPS)):
            near_copy(i, 1).start()
        for h in range(2):
            waiter(zg.at[it, h], a1_ss.at[it], a1_rs.at[it, h]).wait_recv()
            half_copy(h).start()
        for i in range(len(STEPS)):
            near_copy(i, 0).start()

    def gains_in(it):
        waiter(zg.at[it, pl.ds(OWN + 1, 4)], a2_ss.at[it], a2_rs.at[it, 1]).wait_recv()
        waiter(zg.at[it, pl.ds(2, 9)], a2_ss.at[it], a2_rs.at[it, 0]).wait_recv()

    def gains_sent(it):
        waiter(zg.at[it, pl.ds(0, 2)], a1_ss.at[it], a1_rs.at[it, 0]).wait_send()
        waiter(zg.at[it, OWN, pl.ds(0, NS - 1)], a1_ss.at[it], a1_rs.at[it, 0]).wait_send()
        waiter(zg.at[it, pl.ds(0, 13)], a2_ss.at[it], a2_rs.at[it, 0]).wait_send()

    gains_out(0)
    for k in range(NS - 1):
        remote(csend.at[mates[k]], crecv.at[s], c_ss, c_rs.at[s], device(mates[k])).start()
    crecv[s] = csend[s]
    for load in loads[6:]:
        load.wait()
    to_pieces(m_ref, state_m)
    to_pieces(v_ref, state_v)
    gains_on(0)

    sources = [s] + mates[::-1]
    row_id = lax.broadcasted_iota(I32, (ROWS, NBL), 0)

    for i, source in enumerate(sources):
        if i:
            waiter(crecv.at[source], c_ss, c_rs.at[source]).wait_recv()
        for k in range(2):
            row = crecv[source, 134 + k : 135 + k, :].astype(I32)
            pick[:, 256 * i + 128 * k : 256 * i + 128 * k + 128] = jnp.where(row_id == row, 1.0, 0.0).astype(BF16)

    lane32 = lax.broadcasted_iota(I32, (32, 128), 1)
    odd32 = (lane32 & 32) != 0
    odd8 = (lane8 & 32) != 0
    pair32 = lax.broadcasted_iota(I32, (32, 128), 0) >> 2
    chan = 2 * pair32 + jnp.where(odd32, 1, 0)
    a1 = math.exp(-DECAY)

    def decay(steps):
        return jnp.exp(-DECAY * steps.astype(F32))

    whole_chan = chan + 16 * x
    geometric = 1.0 / (1.0 - a1)
    norm = (1.0 - decay(whole_chan + 1)) * geometric + (a1 - decay(NCHAN - whole_chan)) * geometric
    half_norm = BLEND / norm
    from_left = decay(chan + 1)
    from_right = decay(16 - chan)
    near_left = jnp.where(odd32, a1 * a1, a1)
    near_right = jnp.where(odd32, a1, a1 * a1)
    up = jnp.where(odd32, 1.0, a1)
    down = jnp.where(odd32, a1, 1.0)

    def swap(value):
        return jnp.where((lax.broadcasted_iota(I32, value.shape, 1) & 32) != 0, pltpu.roll(value, 32, 1), pltpu.roll(value, 96, 1))

    def smooth(it):
        total = tots[...]
        swapped = swap(total)
        right_going = total * up + swapped * down
        left_going = total * down + swapped * up
        blended = total + a1 * swapped
        zero = jnp.zeros((4, 128), F32)
        lefts, rights = [zero], [zero]
        for k in range(NS):
            lefts.append(a1 * a1 * lefts[-1] + right_going[4 * k : 4 * k + 4])
            q = NS - 1 - k
            rights.append(a1 * a1 * rights[-1] + left_going[4 * q : 4 * q + 4])
        out8 = jnp.concatenate([jnp.where(odd8[0:4], rights[NS], lefts[NS])] * 2, axis=0)
        xs[it] = out8[0:4]
        for dx in (2, 1, 3):
            remote(xs.at[it], xr.at[it, dx - 1], x_ss.at[it], x_rs.at[it], device(s, 0, dx)).start()
        left_all = jnp.concatenate(lefts[:NS], axis=0)
        right_all = jnp.concatenate(rights[NS - 1 :: -1], axis=0)
        blended = blended + near_left * left_all + near_right * right_all
        across = jnp.zeros((4, 128), F32)
        weights = []
        for dx in (1, 2, 3):
            source = lax.rem(x - dx + NX, NX)
            gap = jnp.full((8, 128), jnp.abs(x - source), I32)
            is_left = jnp.full((8, 128), x - source, I32) > 0
            used = jnp.where(is_left, jnp.where(odd8, 0, 1), jnp.where(odd8, 1, 0)).astype(F32)
            weights.append((used * decay(16 * (gap - 1)))[0:4])
        waiter(xr.at[it], x_ss.at[it], x_rs.at[it]).wait_recv()
        for dx in (1, 2, 3):
            across = across + xr[it, dx - 1] * weights[dx - 1]
        across = jnp.concatenate([across] * 8, axis=0)
        other = swap(across)
        blended = blended + from_left * jnp.where(odd32, other, across) + from_right * jnp.where(odd32, across, other)
        return (1.0 - BLEND) * total + half_norm * blended

    coef = -2.0 / math.sqrt(2.0 * NBL * NS * NZ / (4 * NS * NZ))

    for it in range(ITERS):
        last = it == ITERS - 1
        gains_in(it)
        for t in range(4):
            block = zg[it, 4 * t : 4 * t + 4].reshape(128, 128).T
            high = block.astype(BF16)
            gsplit[0:128, 128 * t : 128 * t + 128] = high
            gsplit[128:256, 128 * t : 128 * t + 128] = (block - high.astype(F32)).astype(BF16)

        for i, source in enumerate(sources):
            both = jnp.dot(gsplit[...], pick[:, 256 * i : 256 * i + 256], preferred_element_type=F32)
            both = both[0:128] + both[128:256]
            ga, gb = both[0:64, 0:128], both[64:128, 0:128]
            gc, gd = both[0:64, 128:256], both[64:128, 128:256]
            cr, ci = crecv[source, 0:64, :], crecv[source, 64:128, :]
            u = ga * gc + gb * gd
            v = gb * gc - ga * gd
            model_re = jnp.sum((u * cr - v * ci).reshape(2, SKY_SOURCES, NBL), axis=1)
            model_im = jnp.sum((u * ci + v * cr).reshape(2, SKY_SOURCES, NBL), axis=1)
            weight = crecv[source, 132:134, :]
            err_re = weight * (crecv[source, 128:130, :] - model_re)
            err_im = weight * (crecv[source, 130:132, :] - model_im)
            if last:
                ressend[source] = jnp.concatenate([err_re, err_im], axis=0)
            wide = (2, SKY_SOURCES, NBL)
            sr = jnp.broadcast_to((coef * err_re)[:, None, :], wide).reshape(64, NBL)
            si = jnp.broadcast_to((coef * err_im)[:, None, :], wide).reshape(64, NBL)
            px = gc * cr + gd * ci
            py = gd * cr - gc * ci
            qx = ga * cr - gb * ci
            qy = ga * ci + gb * cr
            terms = ((sr * px - si * py, sr * py + si * px), (sr * qx + si * qy, sr * qy - si * qx))
            for k in range(2):
                for ri in range(2):
                    value = terms[k][ri]
                    high = value.astype(BF16)
                    where = pl.ds(256 * i + 128 * k, 128)
                    grads[64 * ri : 64 * ri + 64, where] = high
                    grads[128 + 64 * ri : 192 + 64 * ri, where] = (value - high.astype(F32)).astype(BF16)

        def station_sums(begin, end):
            both = lax.dot_general(
                pick[begin:end, :], grads[...], (((1,), (1,)), ((), ())), preferred_element_type=F32
            )
            zp[it, begin:end, :] = both[:, 0:128] + both[:, 128:256]

        station_sums(0, 32 * OWN)
        for i, n in enumerate(STEPS):
            remote(zp.at[it, pl.ds(64 + 64 * i, 64)], rsn.at[it, i], r1_ss.at[it], r1_rs.at[it], device(s, -n)).start()
        for h in range(2):
            remote(zp.at[it, pl.ds(320 + 16 * h, 16)], rsh.at[it, h], rh_ss.at[it], rh_rs.at[it], device(s, 6 * h - 3)).start()
        station_sums(32 * OWN, ROWS)
        for i, n in enumerate(STEPS):
            remote(zp.at[it, pl.ds(384 + 32 * i, 32)], rsc.at[it, i], rc_ss.at[it], rc_rs.at[it], device(s, -n)).start()
        if last:
            for k in range(NS - 1):
                remote(ressend.at[mates[k]], resrecv.at[s], o_ss, o_rs, device(mates[k])).start()
            resrecv[s] = ressend[s]
        else:
            waiter(csend.at[pl.ds(0, NS - 1)], c_ss, c_rs.at[s]).wait_send()
        gains_sent(it)
        near = waiter(rsn.at[it], r1_ss.at[it], r1_rs.at[it])
        half = waiter(rsh.at[it], rh_ss.at[it], rh_rs.at[it])
        own = waiter(rsc.at[it], rc_ss.at[it], rc_rs.at[it])
        def far_out(j, acc):
            for k in range(NS):
                accp[it, j, k] = acc[4 * k : 4 * k + 4]
            for k in [*range(NS - 1)] + ([None] if j != 2 else []):
                to = s if k is None else mates[k]
                remote(
                    accp.at[it, j, to], rsp.at[it, j, s], r2_ss.at[it], r2_rs.at[it, j], device(to, CENTRES[j])
                ).start()

        near.wait_recv()
        half.wait_recv()
        acc = zp[it, 0:64, :]
        for i in range(len(STEPS)):
            acc = acc + rsn[it, i]
        far_out(0, jnp.concatenate([acc[0:16] + rsh[it, 0], acc[16:32]], axis=0))
        far_out(1, jnp.concatenate([acc[32:48], acc[48:64] + rsh[it, 1]], axis=0))
        own.wait_recv()
        acc = zp[it, 32 * OWN : 32 * OWN + 32, :]
        for i in range(len(STEPS)):
            acc = acc + rsc[it, i]
        far_out(2, acc)
        rsp[it, 2, s] = accp[it, 2, s]
        near.wait_send()
        half.wait_send()
        own.wait_send()
        if last:
            result = waiter(resrecv.at[pl.ds(0, NS - 1)], o_ss, o_rs)
            result.wait_send()
            result.wait_recv()
            for k in range(NS):
                for ri in range(2):
                    res_ref[ri, 2 * k : 2 * k + 2, :] = resrecv[k, 2 * ri : 2 * ri + 2, :]
        waiter(rsp.at[it, 2, pl.ds(0, NS - 1)], r2_ss.at[it], r2_rs.at[it, 2]).wait_recv()
        for j in range(2):
            waiter(rsp.at[it, j], r2_ss.at[it], r2_rs.at[it, j]).wait_recv()
        for k in range(NS):
            tots[4 * k : 4 * k + 4, :] = rsp[it, 0, k] + rsp[it, 1, k] + rsp[it, 2, k]

        smoothed = smooth(it)
        tally = STEP + it + 1
        new_m = BETA_ONE * state_m[...] + (1.0 - BETA_ONE) * smoothed
        new_v = BETA_TWO * state_v[...] + (1.0 - BETA_TWO) * smoothed * smoothed
        first_hat = new_m / (1.0 - BETA_ONE**tally)
        second_hat = new_v / (1.0 - BETA_TWO**tally)
        new_g = state_g[...] - LEARN_RATE * first_hat / (jnp.sqrt(second_hat) + ADAM_EPSILON)
        if last:
            from_pieces(new_g, go_ref)
            from_pieces(new_m, mo_ref)
            from_pieces(new_v, vo_ref)
        else:
            for k in range(NS):
                gpiece[it + 1, k] = new_g[4 * k : 4 * k + 4]
            gains_out(it + 1)
            state_g[...] = new_g
            state_m[...] = new_m
            state_v[...] = new_v
        waiter(rsp.at[it, pl.ds(0, 2)], r2_ss.at[it], r2_rs.at[it, 0]).wait_send()
        waiter(rsp.at[it, 2, pl.ds(0, NS - 1)], r2_ss.at[it], r2_rs.at[it, 2]).wait_send()
        waiter(xr.at[it], x_ss.at[it], x_rs.at[it]).wait_send()
        if not last:
            gains_on(it + 1)


def store(*refs):
    sem = refs[-1]
    copies = [pltpu.make_async_copy(refs[i], refs[4 + i], sem.at[i]) for i in range(4)]
    for copy in copies:
        copy.start()
    for copy in copies:
        copy.wait()


def on_device(coherency, measured, rejected, pairs, fetch_lists, gains, first, second):
    args = (
        coherency, jnp.swapaxes(measured, 1, 2), rejected.T, pairs.T, fetch_lists.T, gains, first, second,
    )
    args = [pltpu.with_memory_space_constraint(a, pltpu.HBM) for a in args]
    out = [jax.ShapeDtypeStruct(gains.shape, F32)] * 3 + [jax.ShapeDtypeStruct(args[1].shape, F32)]
    vmem = pl.BlockSpec(memory_space=pltpu.VMEM)
    anywhere = pl.BlockSpec(memory_space=pl.ANY)
    hbm = pl.BlockSpec(memory_space=pltpu.HBM)
    sem = pltpu.SemaphoreType.DMA
    buf = pltpu.VMEM
    results = pl.pallas_call(
        kernel,
        out_shape=out,
        in_specs=[hbm] * 8,
        out_specs=[vmem] * 4,
        scratch_shapes=[
            *[buf(a.shape, a.dtype) for a in args],
            sem((8,)),
            buf((NS, CROWS, NBL), F32),
            buf((NS, CROWS, NBL), F32),
            buf((ROWS, 2 * NBL * NS), BF16),
            buf((256, ROWS), BF16),
            buf((256, 2 * NBL * NS), BF16),
            buf((32, 128), F32),
            buf((32, 128), F32),
            buf((32, 128), F32),
            buf((ITERS, NS, 4, 128), F32),
            buf((ITERS, NZ, NS, 4, 128), F32),
            buf((ITERS, ROWS, 128), F32),
            buf((ITERS, 4, 64, 128), F32),
            buf((ITERS, 4, 32, 128), F32),
            buf((ITERS, 2, 16, 128), F32),
            buf((ITERS, 3, NS, 4, 128), F32),
            buf((ITERS, 3, NS, 4, 128), F32),
            buf((32, 128), F32),
            buf((ITERS, 4, 128), F32),
            buf((ITERS, 3, 4, 128), F32),
            buf((NS, 4, 128), F32),
            buf((NS, 4, 128), F32),
            sem, sem((NS,)),
            sem((ITERS,)), sem((ITERS, 3)),
            sem((ITERS,)), sem((ITERS, 2)),
            sem((ITERS,)), sem((ITERS,)),
            sem((ITERS,)), sem((ITERS,)),
            sem((ITERS,)), sem((ITERS,)),
            sem((ITERS,)), sem((ITERS, 3)),
            sem((ITERS,)), sem((ITERS,)),
            sem, sem,
        ],
        compiler_params=pltpu.CompilerParams(collective_id=0, has_side_effects=True, vmem_limit_bytes=32 * 2**20),
        cost_estimate=pl.CostEstimate(flops=4 * 10**9, bytes_accessed=2**20, transcendentals=10**4),
        name="calibrate",
    )(*args)
    new_g, new_m, new_v, residual = pl.pallas_call(
        store, out_shape=out, in_specs=[anywhere] * 4, out_specs=[hbm] * 4, scratch_shapes=[sem((4,))], name="store",
        compiler_params=pltpu.CompilerParams(vmem_limit_bytes=32 * 2**20),
    )(*results)
    return new_g, new_m, new_v, jnp.swapaxes(residual, 1, 2)


def solution(mesh):
    split = P(None, "bl", "ch")
    return jax.shard_map(
        on_device,
        mesh=mesh,
        in_specs=(split, split, P("bl", "ch"), P("bl", None), P(), split, split, split),
        out_specs=(split,) * 4,
        check_vma=False,
    )
```

```python
import math

import jax
import jax.numpy as jnp
from jax import lax
from jax.experimental import pallas as pl
from jax.experimental.pallas import tpu as pltpu
from jax.sharding import PartitionSpec as P

MESH = pl.DeviceIdType.MESH
F32, BF16, I32 = jnp.float32, jnp.bfloat16, jnp.int32

SKY_SOURCES = 32
CELL_READINGS = 16
ITERS = 2
STEP = 3
BETA_ONE = 0.9
BETA_TWO = 0.99
ADAM_EPSILON = 1e-08
LEARN_RATE = 0.3
BLEND = 0.5

NX, NY, NZ, NS = 4, 4, 16, 8
NCHAN = 64
CENTRES = (-6, 6, -3, 3, 0)
STEPS = (1, -1)
ORDER = [-6, 6] + [j - n for n in STEPS for j in (-6, 6)] + [8] + [-3, 3, 0] + [j - n for n in STEPS for j in (-3, 3, 0)]
SLOT = {rel % NZ: slot for slot, rel in enumerate(ORDER)}
OPPOSITE, OWN = 6, 9
FIRST = 7
BACK = (1, 0, 8, 7, OWN)
GROUP = (1, 0, 2, 2, 3)
NC = len(CENTRES)
ROWS = 32 * NZ
PLANE = ((2, 0), (2, 1), (1, 0), (3, 0), (1, 1), (3, 1), (0, 1))
NBL = 128
CROWS = 136
DECAY = 2.0 / NCHAN


def remote(src, dst, send_sem, recv_sem, device):
    return pltpu.make_async_remote_copy(
        src_ref=src, dst_ref=dst, send_sem=send_sem, recv_sem=recv_sem, device_id=device, device_id_type=MESH
    )


def kernel(
    c_hbm, meas_hbm, rej_hbm, pair_hbm, fetch_hbm, g_hbm, m_hbm, v_hbm,
    go_ref, mo_ref, vo_ref, res_ref,
    c_ref, meas_ref, rej_ref, pair_ref, fetch_ref, g_ref, m_ref, v_ref, in_sem,
    csend, crecv, pick, gsplit, grads, state_g, state_m, state_v,
    gpiece, zg, zp, rsn, rsc, rsh, accp, rsp, tots, xs, xr, ressend, resrecv,
    c_ss, c_rs, a1_ss, a1_rs, a2_ss, a2_rs, r1_ss, r1_rs, rc_ss, rc_rs, rh_ss, rh_rs, r2_ss, r2_rs, x_ss, x_rs, o_ss, o_rs,
):
    bl, x = lax.axis_index("bl"), lax.axis_index("ch")
    y, z, c = bl >> 5, (bl >> 1) & (NZ - 1), bl & 1
    s = 2 * y + c
    mates = [2 * ((y + dy) & (NY - 1)) + (c ^ dc) for dy, dc in PLANE]
    plane_at = {dz: 2 * ((z + dz) & (NZ - 1)) for dz in (0, 1, -1, 2, -2, 3, -3, 6, -6)}
    column_of = [32 * ((y + dy) & (NY - 1)) + (c ^ dc) for dy, dc in PLANE] + [32 * y + c]

    def device(k, dz=0, dx=0):
        k = NS - 1 if k is None else k
        return (column_of[k] + plane_at[dz], (x + dx) & (NX - 1) if dx else x)

    barrier = pltpu.get_barrier_semaphore()
    partners = [device(k, j) for j in CENTRES for k in range(NS) if j or k < NS - 1]
    partners += [device(None, n) for n in (2, -2, 1, -1)] + [device(None, 0, dx) for dx in (1, 2, 3)]
    for partner in partners:
        pl.semaphore_signal(barrier, inc=1, device_id=partner, device_id_type=MESH)

    loads = [
        pltpu.make_async_copy(src, dst, in_sem.at[i])
        for i, (src, dst) in enumerate(
            [
                (g_hbm, g_ref), (pair_hbm, pair_ref), (fetch_hbm, fetch_ref), (rej_hbm, rej_ref), (meas_hbm, meas_ref),
                (c_hbm, c_ref), (m_hbm, m_ref), (v_hbm, v_ref),
            ]
        )
    ]
    for load in loads:
        load.start()
    lane8 = lax.broadcasted_iota(I32, (8, 128), 1)
    low8 = lane8 < 64

    def to_pieces(ref, out):
        for t in range(4):
            both = jnp.concatenate([ref[0, :, 128 * t : 128 * t + 128], ref[1, :, 128 * t : 128 * t + 128]], axis=0)
            turned = pltpu.roll(both, 64, 1)
            left = jnp.concatenate([both[0:4], turned[0:4]], axis=0)
            right = jnp.concatenate([turned[4:8], both[4:8]], axis=0)
            out[8 * t : 8 * t + 8, :] = jnp.where(low8, left, right)

    def from_pieces(value, ref):
        for t in range(4):
            both = value[8 * t : 8 * t + 8]
            turned = pltpu.roll(both, 64, 1)
            left = jnp.concatenate([both[0:4], turned[0:4]], axis=0)
            right = jnp.concatenate([turned[4:8], both[4:8]], axis=0)
            mixed = jnp.where(low8, left, right)
            ref[0, :, 128 * t : 128 * t + 128] = mixed[0:4]
            ref[1, :, 128 * t : 128 * t + 128] = mixed[4:8]

    loads[0].wait()
    to_pieces(g_ref, state_g)
    for k in range(NS):
        gpiece[0, k] = state_g[4 * k : 4 * k + 4, :]

    for load in loads[1:5]:
        load.wait()
    fetch = jnp.where(lax.broadcasted_iota(I32, fetch_ref.shape, 1) == bl, fetch_ref[...], 0).astype(F32)
    fetch = jnp.sum(fetch, axis=1, keepdims=True)
    places = lax.broadcasted_iota(I32, (fetch_ref.shape[0], NBL), 0)
    station = jnp.concatenate(
        [
            jnp.sum(jnp.where(places == pair_ref[i : i + 1, :], fetch, 0.0), axis=0, keepdims=True)
            for i in range(2)
        ],
        axis=0,
    ).astype(I32)
    rel = ((station >> 3) & (NZ - 1)) - z
    rel = jnp.where(rel < 0, rel + NZ, rel)
    slot = jnp.zeros_like(rel)
    for k in range(NZ):
        slot = jnp.where(rel == k, SLOT[k], slot)
    weights = (CELL_READINGS - rej_ref[...]).astype(F32) / CELL_READINGS
    rows = (slot * 32 + (station >> 7) * 8 + (station & 7)).astype(F32)
    loads[5].wait()
    for t in range(4):
        for ri in range(2):
            block = c_ref[ri, :, 128 * t : 128 * t + 128].astype(F32).T
            csend[2 * t, 64 * ri : 64 * ri + 64] = block[0:64]
            csend[2 * t + 1, 64 * ri : 64 * ri + 64] = block[64:128]
    for k in range(NS):
        for ri in range(2):
            csend[k, 128 + 2 * ri : 130 + 2 * ri] = meas_ref[ri, 2 * k : 2 * k + 2, :]
        csend[k, 132:134] = weights[2 * k : 2 * k + 2]
        csend[k, 134:136] = rows

    pl.semaphore_wait(barrier, len(partners))

    def waiter(ref, send_sem, recv_sem):
        return remote(ref, ref, send_sem, recv_sem, device(0))

    def gains_out(it):
        for j in range(NC):
            for k in [*range(NS - 1)] + ([None] if CENTRES[j] else []):
                to = s if k is None else mates[k]
                remote(
                    gpiece.at[it, to], zg.at[it, BACK[j], s], a1_ss.at[it], a1_rs.at[it, GROUP[j]], device(k, CENTRES[j])
                ).start()

    def gains_on(it):
        def near_copy(src, width, dst, part, n):
            remote(
                zg.at[it, pl.ds(src, width)], zg.at[it, pl.ds(dst, width)], a2_ss.at[it], a2_rs.at[it, part], device(None, n)
            ).start()

        zg[it, OWN, s] = gpiece[it, s]
        waiter(zg.at[it, OWN, pl.ds(0, NS - 1)], a1_ss.at[it], a1_rs.at[it, 3]).wait_recv()
        for i, n in enumerate(STEPS):
            near_copy(OWN, 1, 12 + 3 * i, 1, n)
        waiter(zg.at[it, pl.ds(7, 2)], a1_ss.at[it], a1_rs.at[it, 2]).wait_recv()
        for i, n in enumerate(STEPS):
            near_copy(7, 2, 10 + 3 * i, 1, n)
        for h in range(2):
            waiter(zg.at[it, h], a1_ss.at[it], a1_rs.at[it, h]).wait_recv()
            half = pl.ds(4 * h, 4)
            remote(
                zg.at[it, h, half], zg.at[it, OPPOSITE, half], a2_ss.at[it], a2_rs.at[it, 0], device(None, 2 - 4 * h)
            ).start()
        for i, n in enumerate(STEPS):
            near_copy(0, 2, 2 + 2 * i, 0, n)

    def gains_in(it):
        waiter(zg.at[it, pl.ds(10, 6)], a2_ss.at[it], a2_rs.at[it, 1]).wait_recv()
        waiter(zg.at[it, pl.ds(2, 5)], a2_ss.at[it], a2_rs.at[it, 0]).wait_recv()

    def gains_sent(it):
        waiter(zg.at[it, pl.ds(0, 4)], a1_ss.at[it], a1_rs.at[it, 0]).wait_send()
        waiter(zg.at[it, OWN, pl.ds(0, NS - 1)], a1_ss.at[it], a1_rs.at[it, 0]).wait_send()
        waiter(zg.at[it, pl.ds(0, 11)], a2_ss.at[it], a2_rs.at[it, 0]).wait_send()

    gains_out(0)
    for k in range(NS - 1):
        remote(csend.at[mates[k]], crecv.at[s], c_ss, c_rs.at[s], device(k)).start()
    crecv[s] = csend[s]
    for load in loads[6:]:
        load.wait()
    to_pieces(m_ref, state_m)
    to_pieces(v_ref, state_v)
    gains_on(0)

    sources = [s] + mates[::-1]
    row_id = lax.broadcasted_iota(I32, (ROWS, NBL), 0)

    for i, source in enumerate(sources):
        if i:
            waiter(crecv.at[source], c_ss, c_rs.at[source]).wait_recv()
        for k in range(2):
            row = crecv[source, 134 + k : 135 + k, :].astype(I32)
            pick[:, 256 * i + 128 * k : 256 * i + 128 * k + 128] = jnp.where(row_id == row, 1.0, 0.0).astype(BF16)

    lane32 = lax.broadcasted_iota(I32, (32, 128), 1)
    odd32 = (lane32 & 32) != 0
    odd8 = (lane8 & 32) != 0
    pair32 = lax.broadcasted_iota(I32, (32, 128), 0) >> 2
    chan = 2 * pair32 + jnp.where(odd32, 1, 0)
    a1 = math.exp(-DECAY)

    def decay(steps):
        return jnp.exp(-DECAY * steps.astype(F32))

    whole_chan = chan + 16 * x
    geometric = 1.0 / (1.0 - a1)
    norm = (1.0 - decay(whole_chan + 1)) * geometric + (a1 - decay(NCHAN - whole_chan)) * geometric
    half_norm = BLEND / norm
    from_left = decay(chan + 1)
    from_right = decay(16 - chan)
    near_left = jnp.where(odd32, a1 * a1, a1)
    near_right = jnp.where(odd32, a1, a1 * a1)
    up = jnp.where(odd32, 1.0, a1)
    down = jnp.where(odd32, a1, 1.0)
    to_edge = decay(2 * jnp.where(odd32, pair32, NS - 1 - pair32))
    edge_same = jnp.where(odd32, down, up) * to_edge
    edge_other = jnp.where(odd32, up, down) * to_edge
    take_left, take_right = half_norm * from_left, half_norm * from_right
    weights = []
    for dx in (1, 2, 3):
        source = (x - dx) & (NX - 1)
        gap = jnp.full((8, 128), jnp.abs(x - source), I32)
        is_left = jnp.full((8, 128), x - source, I32) > 0
        used = jnp.where(is_left, jnp.where(odd8, 0, 1), jnp.where(odd8, 1, 0)).astype(F32)
        weights.append((used * decay(16 * (gap - 1)))[0:4])

    def swap(value):
        return jnp.where((lax.broadcasted_iota(I32, value.shape, 1) & 32) != 0, pltpu.roll(value, 32, 1), pltpu.roll(value, 96, 1))

    def smooth(it):
        total = tots[...]
        swapped = swap(total)
        edge = total * edge_same + swapped * edge_other
        edge = (edge[0:8] + edge[8:16]) + (edge[16:24] + edge[24:32])
        xs[it] = edge[0:4] + edge[4:8]
        for dx in (2, 1, 3):
            remote(xs.at[it], xr.at[it, dx - 1], x_ss.at[it], x_rs.at[it], device(None, 0, dx)).start()
        right_going = total * up + swapped * down
        left_going = total * down + swapped * up
        zero = jnp.zeros((4, 128), F32)
        lefts, rights = [zero], [zero]
        for k in range(NS - 1):
            lefts.append(a1 * a1 * lefts[-1] + right_going[4 * k : 4 * k + 4])
            q = NS - 1 - k
            rights.append(a1 * a1 * rights[-1] + left_going[4 * q : 4 * q + 4])
        left_all = jnp.concatenate(lefts, axis=0)
        right_all = jnp.concatenate(rights[::-1], axis=0)
        blended = total + a1 * swapped + near_left * left_all + near_right * right_all
        smoothed = (1.0 - BLEND) * total + half_norm * blended
        waiter(xr.at[it], x_ss.at[it], x_rs.at[it]).wait_recv()
        across = xr[it, 0] * weights[0] + xr[it, 1] * weights[1] + xr[it, 2] * weights[2]
        across = jnp.concatenate([across] * 2, axis=0)
        other = swap(across)
        left = jnp.concatenate([jnp.where(odd8, other, across)] * 4, axis=0)
        right = jnp.concatenate([jnp.where(odd8, across, other)] * 4, axis=0)
        return smoothed + take_left * left + take_right * right

    coef = -2.0 / math.sqrt(2.0 * NBL * NS * NZ / (4 * NS * NZ))

    for it in range(ITERS):
        last = it == ITERS - 1
        gains_in(it)
        for t in range(4):
            block = zg[it, 4 * t : 4 * t + 4].reshape(128, 128).T
            high = block.astype(BF16)
            gsplit[0:128, 128 * t : 128 * t + 128] = high
            gsplit[128:256, 128 * t : 128 * t + 128] = (block - high.astype(F32)).astype(BF16)

        for i, source in enumerate(sources):
            both = jnp.dot(gsplit[...], pick[:, 256 * i : 256 * i + 256], preferred_element_type=F32)
            both = both[0:128] + both[128:256]
            ga, gb = both[0:64, 0:128], both[64:128, 0:128]
            gc, gd = both[0:64, 128:256], both[64:128, 128:256]
            cr, ci = crecv[source, 0:64, :], crecv[source, 64:128, :]
            u = ga * gc + gb * gd
            v = gb * gc - ga * gd
            model_re = jnp.sum((u * cr - v * ci).reshape(2, SKY_SOURCES, NBL), axis=1)
            model_im = jnp.sum((u * ci + v * cr).reshape(2, SKY_SOURCES, NBL), axis=1)
            weight = crecv[source, 132:134, :]
            err_re = weight * (crecv[source, 128:130, :] - model_re)
            err_im = weight * (crecv[source, 130:132, :] - model_im)
            if last:
                ressend[source] = jnp.concatenate([err_re, err_im], axis=0)
            wide = (2, SKY_SOURCES, NBL)
            sr = jnp.broadcast_to((coef * err_re)[:, None, :], wide).reshape(64, NBL)
            si = jnp.broadcast_to((coef * err_im)[:, None, :], wide).reshape(64, NBL)
            px = gc * cr + gd * ci
            py = gd * cr - gc * ci
            qx = ga * cr - gb * ci
            qy = ga * ci + gb * cr
            terms = ((sr * px - si * py, sr * py + si * px), (sr * qx + si * qy, sr * qy - si * qx))
            for k in range(2):
                for ri in range(2):
                    value = terms[k][ri]
                    high = value.astype(BF16)
                    where = pl.ds(256 * i + 128 * k, 128)
                    grads[64 * ri : 64 * ri + 64, where] = high
                    grads[128 + 64 * ri : 192 + 64 * ri, where] = (value - high.astype(F32)).astype(BF16)

        def station_sums(begin, end):
            both = lax.dot_general(
                pick[begin:end, :], grads[...], (((1,), (1,)), ((), ())), preferred_element_type=F32
            )
            zp[it, begin:end, :] = both[:, 0:128] + both[:, 128:256]

        station_sums(0, 32 * FIRST)
        for i, n in enumerate(STEPS):
            remote(zp.at[it, pl.ds(64 + 64 * i, 64)], rsn.at[it, i], r1_ss.at[it], r1_rs.at[it], device(None, -n)).start()
        for h in range(2):
            remote(
                zp.at[it, pl.ds(32 * OPPOSITE + 16 * h, 16)], rsh.at[it, h], rh_ss.at[it], rh_rs.at[it], device(None, 4 * h - 2)
            ).start()
        station_sums(32 * FIRST, ROWS)
        for i, n in enumerate(STEPS):
            remote(zp.at[it, pl.ds(320 + 96 * i, 96)], rsc.at[it, i], rc_ss.at[it], rc_rs.at[it], device(None, -n)).start()
        if last:
            for k in range(NS - 1):
                remote(ressend.at[mates[k]], resrecv.at[s], o_ss, o_rs, device(k)).start()
            resrecv[s] = ressend[s]
        else:
            waiter(csend.at[pl.ds(0, NS - 1)], c_ss, c_rs.at[s]).wait_send()
        gains_sent(it)
        near = waiter(rsn.at[it], r1_ss.at[it], r1_rs.at[it])
        half = waiter(rsh.at[it], rh_ss.at[it], rh_rs.at[it])
        own = waiter(rsc.at[it], rc_ss.at[it], rc_rs.at[it])
        def far_out(j, acc):
            for k in range(NS):
                accp[it, j, k] = acc[4 * k : 4 * k + 4]
            for k in [*range(NS - 1)] + ([None] if CENTRES[j] else []):
                to = s if k is None else mates[k]
                remote(
                    accp.at[it, j, to], rsp.at[it, j, s], r2_ss.at[it], r2_rs.at[it, (0, 3, 1, 1, 2)[j]], device(k, CENTRES[j])
                ).start()

        near.wait_recv()
        half.wait_recv()
        acc = zp[it, 0:64, :] + rsn[it, 0] + rsn[it, 1]
        far_out(0, jnp.concatenate([acc[0:16] + rsh[it, 0], acc[16:32]], axis=0))
        far_out(1, jnp.concatenate([acc[32:48], acc[48:64] + rsh[it, 1]], axis=0))
        own.wait_recv()
        acc = zp[it, 32 * FIRST : 32 * FIRST + 96, :] + rsc[it, 0] + rsc[it, 1]
        for j in (2, 3, 4):
            far_out(j, acc[32 * j - 64 : 32 * j - 32])
        rsp[it, NC - 1, s] = accp[it, NC - 1, s]
        near.wait_send()
        half.wait_send()
        own.wait_send()
        if last:
            result = waiter(resrecv.at[pl.ds(0, NS - 1)], o_ss, o_rs)
            result.wait_send()
            result.wait_recv()
            for k in range(NS):
                for ri in range(2):
                    res_ref[ri, 2 * k : 2 * k + 2, :] = resrecv[k, 2 * ri : 2 * ri + 2, :]
        waiter(rsp.at[it, NC - 1, pl.ds(0, NS - 1)], r2_ss.at[it], r2_rs.at[it, 2]).wait_recv()
        waiter(rsp.at[it, pl.ds(2, 2)], r2_ss.at[it], r2_rs.at[it, 1]).wait_recv()
        for k in range(NS):
            tots[4 * k : 4 * k + 4, :] = rsp[it, 4, k] + rsp[it, 2, k] + rsp[it, 3, k]
        for j in (0, 1):
            waiter(rsp.at[it, j], r2_ss.at[it], r2_rs.at[it, j and 3]).wait_recv()
        for k in range(NS):
            tots[4 * k : 4 * k + 4, :] += rsp[it, 0, k] + rsp[it, 1, k]

        smoothed = smooth(it)
        tally = STEP + it + 1
        new_m = BETA_ONE * state_m[...] + (1.0 - BETA_ONE) * smoothed
        new_v = BETA_TWO * state_v[...] + (1.0 - BETA_TWO) * smoothed * smoothed
        first_hat = new_m / (1.0 - BETA_ONE**tally)
        second_hat = new_v / (1.0 - BETA_TWO**tally)
        new_g = state_g[...] - LEARN_RATE * first_hat / (jnp.sqrt(second_hat) + ADAM_EPSILON)
        if last:
            from_pieces(new_g, go_ref)
            from_pieces(new_m, mo_ref)
            from_pieces(new_v, vo_ref)
        else:
            for k in range(NS):
                gpiece[it + 1, k] = new_g[4 * k : 4 * k + 4]
            gains_out(it + 1)
            state_g[...] = new_g
            state_m[...] = new_m
            state_v[...] = new_v
        waiter(rsp.at[it, pl.ds(0, NC - 1)], r2_ss.at[it], r2_rs.at[it, 0]).wait_send()
        waiter(rsp.at[it, NC - 1, pl.ds(0, NS - 1)], r2_ss.at[it], r2_rs.at[it, 2]).wait_send()
        waiter(xr.at[it], x_ss.at[it], x_rs.at[it]).wait_send()
        if not last:
            gains_on(it + 1)


def store(*refs):
    sem = refs[-1]
    copies = [pltpu.make_async_copy(refs[i], refs[4 + i], sem.at[i]) for i in range(4)]
    for copy in copies:
        copy.start()
    for copy in copies:
        copy.wait()


def on_device(coherency, measured, rejected, pairs, fetch_lists, gains, first, second):
    args = (
        coherency, jnp.swapaxes(measured, 1, 2), rejected.T, pairs.T, fetch_lists.T, gains, first, second,
    )
    args = [pltpu.with_memory_space_constraint(a, pltpu.HBM) for a in args]
    out = [jax.ShapeDtypeStruct(gains.shape, F32)] * 3 + [jax.ShapeDtypeStruct(args[1].shape, F32)]
    vmem = pl.BlockSpec(memory_space=pltpu.VMEM)
    anywhere = pl.BlockSpec(memory_space=pl.ANY)
    hbm = pl.BlockSpec(memory_space=pltpu.HBM)
    sem = pltpu.SemaphoreType.DMA
    buf = pltpu.VMEM
    results = pl.pallas_call(
        kernel,
        out_shape=out,
        in_specs=[hbm] * 8,
        out_specs=[vmem] * 4,
        scratch_shapes=[
            *[buf(a.shape, a.dtype) for a in args],
            sem((8,)),
            buf((NS, CROWS, NBL), F32),
            buf((NS, CROWS, NBL), F32),
            buf((ROWS, 2 * NBL * NS), BF16),
            buf((256, ROWS), BF16),
            buf((256, 2 * NBL * NS), BF16),
            buf((32, 128), F32),
            buf((32, 128), F32),
            buf((32, 128), F32),
            buf((ITERS, NS, 4, 128), F32),
            buf((ITERS, NZ, NS, 4, 128), F32),
            buf((ITERS, ROWS, 128), F32),
            buf((ITERS, 2, 64, 128), F32),
            buf((ITERS, 2, 96, 128), F32),
            buf((ITERS, 2, 16, 128), F32),
            buf((ITERS, NC, NS, 4, 128), F32),
            buf((ITERS, NC, NS, 4, 128), F32),
            buf((32, 128), F32),
            buf((ITERS, 4, 128), F32),
            buf((ITERS, 3, 4, 128), F32),
            buf((NS, 4, 128), F32),
            buf((NS, 4, 128), F32),
            sem, sem((NS,)),
            sem((ITERS,)), sem((ITERS, 4)),
            sem((ITERS,)), sem((ITERS, 2)),
            sem((ITERS,)), sem((ITERS,)),
            sem((ITERS,)), sem((ITERS,)),
            sem((ITERS,)), sem((ITERS,)),
            sem((ITERS,)), sem((ITERS, 4)),
            sem((ITERS,)), sem((ITERS,)),
            sem, sem,
        ],
        compiler_params=pltpu.CompilerParams(collective_id=0, has_side_effects=True, vmem_limit_bytes=32 * 2**20),
        cost_estimate=pl.CostEstimate(flops=4 * 10**9, bytes_accessed=2**20, transcendentals=10**4),
        name="calibrate",
    )(*args)
    new_g, new_m, new_v, residual = pl.pallas_call(
        store, out_shape=out, in_specs=[anywhere] * 4, out_specs=[hbm] * 4, scratch_shapes=[sem((4,))], name="store",
        compiler_params=pltpu.CompilerParams(vmem_limit_bytes=32 * 2**20),
    )(*results)
    return new_g, new_m, new_v, jnp.swapaxes(residual, 1, 2)


def solution(mesh):
    split = P(None, "bl", "ch")
    return jax.shard_map(
        on_device,
        mesh=mesh,
        in_specs=(split, split, P("bl", "ch"), P("bl", None), P(), split, split, split),
        out_specs=(split,) * 4,
        check_vma=False,
    )
```

```python
import math

import jax
import jax.numpy as jnp
from jax import lax
from jax.experimental import pallas as pl
from jax.experimental.pallas import tpu as pltpu
from jax.sharding import PartitionSpec as P

MESH = pl.DeviceIdType.MESH
F32, BF16, I32 = jnp.float32, jnp.bfloat16, jnp.int32

SKY_SOURCES = 32
CELL_READINGS = 16
ITERS = 2
STEP = 3
BETA_ONE = 0.9
BETA_TWO = 0.99
ADAM_EPSILON = 1e-08
LEARN_RATE = 0.3
BLEND = 0.5

NX, NY, NZ, NS = 4, 4, 16, 8
NCHAN = 64
CENTRES = (-6, 6, -3, 3, 0)
STEPS = (1, -1)
ORDER = [-6, 6] + [j - n for n in STEPS for j in (-6, 6)] + [8] + [-3, 3, 0] + [j - n for n in STEPS for j in (-3, 3, 0)]
SLOT = {rel % NZ: slot for slot, rel in enumerate(ORDER)}
OPPOSITE, OWN = 6, 9
FIRST = 7
BACK = (1, 0, 8, 7, OWN)
GROUP = (1, 0, 2, 2, 3)
NC = len(CENTRES)
ROWS = 32 * NZ
PLANE = ((2, 0), (2, 1), (1, 0), (3, 0), (1, 1), (3, 1), (0, 1))
NBL = 128
CROWS = 136
DECAY = 2.0 / NCHAN


def remote(src, dst, send_sem, recv_sem, device):
    return pltpu.make_async_remote_copy(
        src_ref=src, dst_ref=dst, send_sem=send_sem, recv_sem=recv_sem, device_id=device, device_id_type=MESH
    )


def kernel(
    c_hbm, meas_hbm, rej_hbm, pair_hbm, fetch_hbm, g_hbm, m_hbm, v_hbm,
    go_ref, mo_ref, vo_ref, res_ref,
    c_ref, meas_ref, rej_ref, pair_ref, fetch_ref, g_ref, m_ref, v_ref, in_sem,
    csend, crecv, pick, gsplit, early, grads, state_g, state_m, state_v,
    gpiece, zg, zp, rsn, rsc, rsh, accp, rsp, tots, xs, xr, ressend, resrecv,
    c_ss, c_rs, a1_ss, a1_rs, a2_ss, a2_rs, r1_ss, r1_rs, rc_ss, rc_rs, rh_ss, rh_rs, r2_ss, r2_rs, x_ss, x_rs, o_ss, o_rs,
):
    bl, x = lax.axis_index("bl"), lax.axis_index("ch")
    y, z, c = bl >> 5, (bl >> 1) & (NZ - 1), bl & 1
    s = 2 * y + c
    mates = [2 * ((y + dy) & (NY - 1)) + (c ^ dc) for dy, dc in PLANE]
    plane_at = {dz: 2 * ((z + dz) & (NZ - 1)) for dz in (0, 1, -1, 2, -2, 3, -3, 6, -6)}
    column_of = [32 * ((y + dy) & (NY - 1)) + (c ^ dc) for dy, dc in PLANE] + [32 * y + c]

    def device(k, dz=0, dx=0):
        k = NS - 1 if k is None else k
        return (column_of[k] + plane_at[dz], (x + dx) & (NX - 1) if dx else x)

    toward = jnp.where((z >= 1) & (z <= NZ // 2), 0, 1)

    def device_along(k, direction, planes):
        k = NS - 1 if k is None else k
        return (column_of[k] + 2 * ((z + planes * (2 * direction - 1)) & (NZ - 1)), x)

    barrier = pltpu.get_barrier_semaphore()
    partners = [device(k, j) for j in CENTRES for k in range(NS) if j or k < NS - 1]
    partners += [device(None, n) for n in (2, -2, 1, -1)] + [device(None, 0, dx) for dx in (1, 2, 3)]
    for partner in partners:
        pl.semaphore_signal(barrier, inc=1, device_id=partner, device_id_type=MESH)

    loads = [
        pltpu.make_async_copy(src, dst, in_sem.at[i])
        for i, (src, dst) in enumerate(
            [
                (g_hbm, g_ref), (pair_hbm, pair_ref), (fetch_hbm, fetch_ref), (rej_hbm, rej_ref), (meas_hbm, meas_ref),
                (c_hbm, c_ref), (m_hbm, m_ref), (v_hbm, v_ref),
            ]
        )
    ]
    for load in loads:
        load.start()
    lane8 = lax.broadcasted_iota(I32, (8, 128), 1)
    low8 = lane8 < 64

    def to_pieces(ref, out):
        for t in range(4):
            both = jnp.concatenate([ref[0, :, 128 * t : 128 * t + 128], ref[1, :, 128 * t : 128 * t + 128]], axis=0)
            turned = pltpu.roll(both, 64, 1)
            left = jnp.concatenate([both[0:4], turned[0:4]], axis=0)
            right = jnp.concatenate([turned[4:8], both[4:8]], axis=0)
            out[8 * t : 8 * t + 8, :] = jnp.where(low8, left, right)

    def from_pieces(value, ref):
        for t in range(4):
            both = value[8 * t : 8 * t + 8]
            turned = pltpu.roll(both, 64, 1)
            left = jnp.concatenate([both[0:4], turned[0:4]], axis=0)
            right = jnp.concatenate([turned[4:8], both[4:8]], axis=0)
            mixed = jnp.where(low8, left, right)
            ref[0, :, 128 * t : 128 * t + 128] = mixed[0:4]
            ref[1, :, 128 * t : 128 * t + 128] = mixed[4:8]

    loads[0].wait()
    to_pieces(g_ref, state_g)
    for k in range(NS):
        gpiece[0, k] = state_g[4 * k : 4 * k + 4, :]

    for load in loads[1:5]:
        load.wait()
    fetch = jnp.where(lax.broadcasted_iota(I32, fetch_ref.shape, 1) == bl, fetch_ref[...], 0).astype(F32)
    fetch = jnp.sum(fetch, axis=1, keepdims=True)
    places = lax.broadcasted_iota(I32, (fetch_ref.shape[0], NBL), 0)
    station = jnp.concatenate(
        [
            jnp.sum(jnp.where(places == pair_ref[i : i + 1, :], fetch, 0.0), axis=0, keepdims=True)
            for i in range(2)
        ],
        axis=0,
    ).astype(I32)
    rel = ((station >> 3) & (NZ - 1)) - z
    rel = jnp.where(rel < 0, rel + NZ, rel)
    slot = jnp.zeros_like(rel)
    for k in range(NZ):
        slot = jnp.where(rel == k, SLOT[k], slot)
    weights = (CELL_READINGS - rej_ref[...]).astype(F32) / CELL_READINGS
    rows = (slot * 32 + (station >> 7) * 8 + (station & 7)).astype(F32)
    loads[5].wait()
    for t in range(4):
        for ri in range(2):
            block = c_ref[ri, :, 128 * t : 128 * t + 128].astype(F32).T
            csend[2 * t, 64 * ri : 64 * ri + 64] = block[0:64]
            csend[2 * t + 1, 64 * ri : 64 * ri + 64] = block[64:128]
    for k in range(NS):
        for ri in range(2):
            csend[k, 128 + 2 * ri : 130 + 2 * ri] = meas_ref[ri, 2 * k : 2 * k + 2, :]
        csend[k, 132:134] = weights[2 * k : 2 * k + 2]
        csend[k, 134:136] = rows

    pl.semaphore_wait(barrier, len(partners))

    def waiter(ref, send_sem, recv_sem):
        return remote(ref, ref, send_sem, recv_sem, device(0))

    def gains_out(it):
        for j in range(NC):
            for k in [*range(NS - 1)] + ([None] if CENTRES[j] else []):
                to = s if k is None else mates[k]
                remote(
                    gpiece.at[it, to], zg.at[it, BACK[j], s], a1_ss.at[it], a1_rs.at[it, GROUP[j]], device(k, CENTRES[j])
                ).start()

    def gains_on(it):
        def near_copy(src, width, dst, part, n):
            remote(
                zg.at[it, pl.ds(src, width)], zg.at[it, pl.ds(dst, width)], a2_ss.at[it], a2_rs.at[it, part], device(None, n)
            ).start()

        zg[it, OWN, s] = gpiece[it, s]
        waiter(zg.at[it, OWN, pl.ds(0, NS - 1)], a1_ss.at[it], a1_rs.at[it, 3]).wait_recv()
        for i, n in enumerate(STEPS):
            near_copy(OWN, 1, 12 + 3 * i, 1, n)
        waiter(zg.at[it, pl.ds(7, 2)], a1_ss.at[it], a1_rs.at[it, 2]).wait_recv()
        for i, n in enumerate(STEPS):
            near_copy(7, 2, 10 + 3 * i, 1, n)
        for h in range(2):
            waiter(zg.at[it, h], a1_ss.at[it], a1_rs.at[it, h]).wait_recv()
            half = pl.ds(4 * h, 4)
            remote(
                zg.at[it, h, half], zg.at[it, OPPOSITE, half], a2_ss.at[it], a2_rs.at[it, 0], device(None, 2 - 4 * h)
            ).start()
        for i, n in enumerate(STEPS):
            near_copy(0, 2, 2 + 2 * i, 0, n)

    def gains_in(it, part):
        slots = pl.ds(10, 6) if part else pl.ds(2, 5)
        waiter(zg.at[it, slots], a2_ss.at[it], a2_rs.at[it, part]).wait_recv()

    def gains_sent(it):
        waiter(zg.at[it, pl.ds(0, 4)], a1_ss.at[it], a1_rs.at[it, 0]).wait_send()
        waiter(zg.at[it, OWN, pl.ds(0, NS - 1)], a1_ss.at[it], a1_rs.at[it, 0]).wait_send()
        waiter(zg.at[it, pl.ds(0, 11)], a2_ss.at[it], a2_rs.at[it, 0]).wait_send()

    gains_out(0)
    for k in range(NS - 1):
        remote(csend.at[mates[k]], crecv.at[s], c_ss, c_rs.at[s], device(k)).start()
    crecv[s] = csend[s]
    for load in loads[6:]:
        load.wait()
    to_pieces(m_ref, state_m)
    to_pieces(v_ref, state_v)
    gains_on(0)

    sources = [s] + mates[::-1]
    row_id = lax.broadcasted_iota(I32, (ROWS, NBL), 0)

    for i, source in enumerate(sources):
        if i:
            waiter(crecv.at[source], c_ss, c_rs.at[source]).wait_recv()
        for k in range(2):
            row = crecv[source, 134 + k : 135 + k, :].astype(I32)
            pick[:, 256 * i + 128 * k : 256 * i + 128 * k + 128] = jnp.where(row_id == row, 1.0, 0.0).astype(BF16)

    lane32 = lax.broadcasted_iota(I32, (32, 128), 1)
    odd32 = (lane32 & 32) != 0
    odd8 = (lane8 & 32) != 0
    pair32 = lax.broadcasted_iota(I32, (32, 128), 0) >> 2
    chan = 2 * pair32 + jnp.where(odd32, 1, 0)
    a1 = math.exp(-DECAY)

    def decay(steps):
        return jnp.exp(-DECAY * steps.astype(F32))

    whole_chan = chan + 16 * x
    geometric = 1.0 / (1.0 - a1)
    norm = (1.0 - decay(whole_chan + 1)) * geometric + (a1 - decay(NCHAN - whole_chan)) * geometric
    half_norm = BLEND / norm
    from_left = decay(chan + 1)
    from_right = decay(16 - chan)
    near_left = jnp.where(odd32, a1 * a1, a1)
    near_right = jnp.where(odd32, a1, a1 * a1)
    up = jnp.where(odd32, 1.0, a1)
    down = jnp.where(odd32, a1, 1.0)
    to_edge = decay(2 * jnp.where(odd32, pair32, NS - 1 - pair32))
    edge_same = jnp.where(odd32, down, up) * to_edge
    edge_other = jnp.where(odd32, up, down) * to_edge
    take_left, take_right = half_norm * from_left, half_norm * from_right
    weights = []
    for dx in (1, 2, 3):
        source = (x - dx) & (NX - 1)
        gap = jnp.full((8, 128), jnp.abs(x - source), I32)
        is_left = jnp.full((8, 128), x - source, I32) > 0
        used = jnp.where(is_left, jnp.where(odd8, 0, 1), jnp.where(odd8, 1, 0)).astype(F32)
        weights.append((used * decay(16 * (gap - 1)))[0:4])

    def swap(value):
        return jnp.where((lax.broadcasted_iota(I32, value.shape, 1) & 32) != 0, pltpu.roll(value, 32, 1), pltpu.roll(value, 96, 1))

    def smooth(it):
        total = tots[...]
        swapped = swap(total)
        edge = total * edge_same + swapped * edge_other
        edge = (edge[0:8] + edge[8:16]) + (edge[16:24] + edge[24:32])
        xs[it] = edge[0:4] + edge[4:8]
        for dx in (2, 1, 3):
            remote(xs.at[it], xr.at[it, dx - 1], x_ss.at[it], x_rs.at[it], device(None, 0, dx)).start()
        right_going = total * up + swapped * down
        left_going = total * down + swapped * up
        zero = jnp.zeros((4, 128), F32)
        lefts, rights = [zero], [zero]
        for k in range(NS - 1):
            lefts.append(a1 * a1 * lefts[-1] + right_going[4 * k : 4 * k + 4])
            q = NS - 1 - k
            rights.append(a1 * a1 * rights[-1] + left_going[4 * q : 4 * q + 4])
        left_all = jnp.concatenate(lefts, axis=0)
        right_all = jnp.concatenate(rights[::-1], axis=0)
        blended = total + a1 * swapped + near_left * left_all + near_right * right_all
        smoothed = (1.0 - BLEND) * total + half_norm * blended
        waiter(xr.at[it], x_ss.at[it], x_rs.at[it]).wait_recv()
        across = xr[it, 0] * weights[0] + xr[it, 1] * weights[1] + xr[it, 2] * weights[2]
        across = jnp.concatenate([across] * 2, axis=0)
        other = swap(across)
        left = jnp.concatenate([jnp.where(odd8, other, across)] * 4, axis=0)
        right = jnp.concatenate([jnp.where(odd8, across, other)] * 4, axis=0)
        return smoothed + take_left * left + take_right * right

    coef = -2.0 / math.sqrt(2.0 * NBL * NS * NZ / (4 * NS * NZ))

    for it in range(ITERS):
        last = it == ITERS - 1
        def split(t):
            block = zg[it, 4 * t : 4 * t + 4].reshape(128, 128).T
            high = block.astype(BF16)
            gsplit[0:128, 128 * t : 128 * t + 128] = high
            gsplit[128:256, 128 * t : 128 * t + 128] = (block - high.astype(F32)).astype(BF16)

        gains_in(it, 1)
        split(2)
        split(3)
        for i in range(NS):
            both = jnp.dot(gsplit[:, 256:512], pick[256:512, 256 * i : 256 * i + 256], preferred_element_type=F32)
            early[i] = both[0:128] + both[128:256]
        gains_in(it, 0)
        split(0)
        split(1)
        for i, source in enumerate(sources):
            both = jnp.dot(gsplit[:, 0:256], pick[0:256, 256 * i : 256 * i + 256], preferred_element_type=F32)
            both = both[0:128] + both[128:256] + early[i]
            ga, gb = both[0:64, 0:128], both[64:128, 0:128]
            gc, gd = both[0:64, 128:256], both[64:128, 128:256]
            cr, ci = crecv[source, 0:64, :], crecv[source, 64:128, :]
            u = ga * gc + gb * gd
            v = gb * gc - ga * gd
            model_re = jnp.sum((u * cr - v * ci).reshape(2, SKY_SOURCES, NBL), axis=1)
            model_im = jnp.sum((u * ci + v * cr).reshape(2, SKY_SOURCES, NBL), axis=1)
            weight = crecv[source, 132:134, :]
            err_re = weight * (crecv[source, 128:130, :] - model_re)
            err_im = weight * (crecv[source, 130:132, :] - model_im)
            if last:
                ressend[source] = jnp.concatenate([err_re, err_im], axis=0)
            wide = (2, SKY_SOURCES, NBL)
            sr = jnp.broadcast_to((coef * err_re)[:, None, :], wide).reshape(64, NBL)
            si = jnp.broadcast_to((coef * err_im)[:, None, :], wide).reshape(64, NBL)
            px = gc * cr + gd * ci
            py = gd * cr - gc * ci
            qx = ga * cr - gb * ci
            qy = ga * ci + gb * cr
            terms = ((sr * px - si * py, sr * py + si * px), (sr * qx + si * qy, sr * qy - si * qx))
            for k in range(2):
                for ri in range(2):
                    value = terms[k][ri]
                    high = value.astype(BF16)
                    where = pl.ds(256 * i + 128 * k, 128)
                    grads[64 * ri : 64 * ri + 64, where] = high
                    grads[128 + 64 * ri : 192 + 64 * ri, where] = (value - high.astype(F32)).astype(BF16)

        def station_sums(begin, end):
            both = lax.dot_general(
                pick[begin:end, :], grads[...], (((1,), (1,)), ((), ())), preferred_element_type=F32
            )
            zp[it, begin:end, :] = both[:, 0:128] + both[:, 128:256]

        station_sums(0, 32 * FIRST)
        for h in range(2):
            remote(
                zp.at[it, pl.ds(32 * OPPOSITE + 16 * h, 16)], rsh.at[it, h], rh_ss.at[it], rh_rs.at[it], device(None, 4 * h - 2)
            ).start()
        for i in (toward, 1 - toward):
            rows = pl.ds(pl.multiple_of(64 + 64 * i, 32), 64)
            remote(zp.at[it, rows], rsn.at[it, i], r1_ss.at[it], r1_rs.at[it], device_along(None, i, 1)).start()
        station_sums(32 * FIRST, ROWS)
        for i in (toward, 1 - toward):
            rows = pl.ds(pl.multiple_of(320 + 96 * i, 32), 96)
            remote(zp.at[it, rows], rsc.at[it, i], rc_ss.at[it], rc_rs.at[it], device_along(None, i, 1)).start()
        if last:
            for k in range(NS - 1):
                remote(ressend.at[mates[k]], resrecv.at[s], o_ss, o_rs, device(k)).start()
            resrecv[s] = ressend[s]
        else:
            waiter(csend.at[pl.ds(0, NS - 1)], c_ss, c_rs.at[s]).wait_send()
        gains_sent(it)
        near = waiter(rsn.at[it], r1_ss.at[it], r1_rs.at[it])
        half = waiter(rsh.at[it], rh_ss.at[it], rh_rs.at[it])
        own = waiter(rsc.at[it], rc_ss.at[it], rc_rs.at[it])
        def far_store(j, acc):
            for k in range(NS):
                accp[it, j, k] = acc[4 * k : 4 * k + 4]

        def far_out(planes):
            first = 0 if planes == 6 else 2
            for side in (toward, 1 - toward):
                j = first + side
                for k in [*range(NS - 1), None]:
                    to = s if k is None else mates[k]
                    remote(
                        accp.at[it, j, to], rsp.at[it, j, s], r2_ss.at[it], r2_rs.at[it, j], device_along(k, side, planes)
                    ).start()

        near.wait_recv()
        half.wait_recv()
        acc = zp[it, 0:64, :] + rsn[it, 0] + rsn[it, 1]
        far_store(0, jnp.concatenate([acc[0:16] + rsh[it, 0], acc[16:32]], axis=0))
        far_store(1, jnp.concatenate([acc[32:48], acc[48:64] + rsh[it, 1]], axis=0))
        far_out(6)
        own.wait_recv()
        acc = zp[it, 32 * FIRST : 32 * FIRST + 96, :] + rsc[it, 0] + rsc[it, 1]
        for j in (2, 3, 4):
            far_store(j, acc[32 * j - 64 : 32 * j - 32])
        far_out(3)
        for k in range(NS - 1):
            remote(
                accp.at[it, NC - 1, mates[k]], rsp.at[it, NC - 1, s], r2_ss.at[it], r2_rs.at[it, NC - 1], device(k)
            ).start()
        rsp[it, NC - 1, s] = accp[it, NC - 1, s]
        near.wait_send()
        half.wait_send()
        own.wait_send()
        if last:
            result = waiter(resrecv.at[pl.ds(0, NS - 1)], o_ss, o_rs)
            result.wait_send()
            result.wait_recv()
            for k in range(NS):
                for ri in range(2):
                    res_ref[ri, 2 * k : 2 * k + 2, :] = resrecv[k, 2 * ri : 2 * ri + 2, :]
        waiter(rsp.at[it, NC - 1, pl.ds(0, NS - 1)], r2_ss.at[it], r2_rs.at[it, NC - 1]).wait_recv()
        for j in (2, 3):
            waiter(rsp.at[it, j], r2_ss.at[it], r2_rs.at[it, j]).wait_recv()
        for k in range(NS):
            tots[4 * k : 4 * k + 4, :] = rsp[it, 4, k] + rsp[it, 2, k] + rsp[it, 3, k]
        for j in (0, 1):
            waiter(rsp.at[it, j], r2_ss.at[it], r2_rs.at[it, j]).wait_recv()
        for k in range(NS):
            tots[4 * k : 4 * k + 4, :] += rsp[it, 0, k] + rsp[it, 1, k]

        smoothed = smooth(it)
        tally = STEP + it + 1
        new_m = BETA_ONE * state_m[...] + (1.0 - BETA_ONE) * smoothed
        new_v = BETA_TWO * state_v[...] + (1.0 - BETA_TWO) * smoothed * smoothed
        rate = LEARN_RATE / (1.0 - BETA_ONE**tally)
        new_g = state_g[...] - rate * new_m / (jnp.sqrt(new_v * (1.0 / (1.0 - BETA_TWO**tally))) + ADAM_EPSILON)
        if last:
            from_pieces(new_g, go_ref)
            from_pieces(new_m, mo_ref)
            from_pieces(new_v, vo_ref)
        else:
            for k in range(NS):
                gpiece[it + 1, k] = new_g[4 * k : 4 * k + 4]
            gains_out(it + 1)
            state_g[...] = new_g
            state_m[...] = new_m
            state_v[...] = new_v
        waiter(rsp.at[it, pl.ds(0, NC - 1)], r2_ss.at[it], r2_rs.at[it, 0]).wait_send()
        waiter(rsp.at[it, NC - 1, pl.ds(0, NS - 1)], r2_ss.at[it], r2_rs.at[it, 2]).wait_send()
        waiter(xr.at[it], x_ss.at[it], x_rs.at[it]).wait_send()
        if not last:
            gains_on(it + 1)


def store(*refs):
    sem = refs[-1]
    copies = [pltpu.make_async_copy(refs[i], refs[4 + i], sem.at[i]) for i in range(4)]
    for copy in copies:
        copy.start()
    for copy in copies:
        copy.wait()


def on_device(coherency, measured, rejected, pairs, fetch_lists, gains, first, second):
    args = (
        coherency, jnp.swapaxes(measured, 1, 2), rejected.T, pairs.T, fetch_lists.T, gains, first, second,
    )
    args = [pltpu.with_memory_space_constraint(a, pltpu.HBM) for a in args]
    out = [jax.ShapeDtypeStruct(gains.shape, F32)] * 3 + [jax.ShapeDtypeStruct(args[1].shape, F32)]
    vmem = pl.BlockSpec(memory_space=pltpu.VMEM)
    anywhere = pl.BlockSpec(memory_space=pl.ANY)
    hbm = pl.BlockSpec(memory_space=pltpu.HBM)
    sem = pltpu.SemaphoreType.DMA
    buf = pltpu.VMEM
    results = pl.pallas_call(
        kernel,
        out_shape=out,
        in_specs=[hbm] * 8,
        out_specs=[vmem] * 4,
        scratch_shapes=[
            *[buf(a.shape, a.dtype) for a in args],
            sem((8,)),
            buf((NS, CROWS, NBL), F32),
            buf((NS, CROWS, NBL), F32),
            buf((ROWS, 2 * NBL * NS), BF16),
            buf((256, ROWS), BF16),
            buf((NS, 128, 256), F32),
            buf((256, 2 * NBL * NS), BF16),
            buf((32, 128), F32),
            buf((32, 128), F32),
            buf((32, 128), F32),
            buf((ITERS, NS, 4, 128), F32),
            buf((ITERS, NZ, NS, 4, 128), F32),
            buf((ITERS, ROWS, 128), F32),
            buf((ITERS, 2, 64, 128), F32),
            buf((ITERS, 2, 96, 128), F32),
            buf((ITERS, 2, 16, 128), F32),
            buf((ITERS, NC, NS, 4, 128), F32),
            buf((ITERS, NC, NS, 4, 128), F32),
            buf((32, 128), F32),
            buf((ITERS, 4, 128), F32),
            buf((ITERS, 3, 4, 128), F32),
            buf((NS, 4, 128), F32),
            buf((NS, 4, 128), F32),
            sem, sem((NS,)),
            sem((ITERS,)), sem((ITERS, 4)),
            sem((ITERS,)), sem((ITERS, 2)),
            sem((ITERS,)), sem((ITERS,)),
            sem((ITERS,)), sem((ITERS,)),
            sem((ITERS,)), sem((ITERS,)),
            sem((ITERS,)), sem((ITERS, NC)),
            sem((ITERS,)), sem((ITERS,)),
            sem, sem,
        ],
        compiler_params=pltpu.CompilerParams(collective_id=0, has_side_effects=True, vmem_limit_bytes=32 * 2**20),
        cost_estimate=pl.CostEstimate(flops=4 * 10**9, bytes_accessed=2**20, transcendentals=10**4),
        name="calibrate",
    )(*args)
    new_g, new_m, new_v, residual = pl.pallas_call(
        store, out_shape=out, in_specs=[anywhere] * 4, out_specs=[hbm] * 4, scratch_shapes=[sem((4,))], name="store",
        compiler_params=pltpu.CompilerParams(vmem_limit_bytes=32 * 2**20),
    )(*results)
    return new_g, new_m, new_v, jnp.swapaxes(residual, 1, 2)


def solution(mesh):
    split = P(None, "bl", "ch")
    return jax.shard_map(
        on_device,
        mesh=mesh,
        in_specs=(split, split, P("bl", "ch"), P("bl", None), P(), split, split, split),
        out_specs=(split,) * 4,
        check_vma=False,
    )
```

```python
import math

import jax
import jax.numpy as jnp
from jax import lax
from jax.experimental import pallas as pl
from jax.experimental.pallas import tpu as pltpu
from jax.sharding import PartitionSpec as P

MESH = pl.DeviceIdType.MESH
F32, BF16, I32 = jnp.float32, jnp.bfloat16, jnp.int32

SKY_SOURCES = 32
CELL_READINGS = 16
ITERS = 2
STEP = 3
BETA_ONE = 0.9
BETA_TWO = 0.99
ADAM_EPSILON = 1e-08
LEARN_RATE = 0.3
BLEND = 0.5

NX, NY, NZ, NS = 4, 4, 16, 8
NCHAN = 64
CENTRES = (-6, 6, -3, 3, 0)
STEPS = (1, -1)
ORDER = [-6, 6] + [j - n for n in STEPS for j in (-6, 6)] + [8] + [-3, 3, 0] + [j - n for n in STEPS for j in (-3, 3, 0)]
SLOT = {rel % NZ: slot for slot, rel in enumerate(ORDER)}
OPPOSITE, OWN = 6, 9
FIRST = 7
BACK = (1, 0, 8, 7, OWN)
GROUP = (1, 0, 2, 2, 3)
NC = len(CENTRES)
ROWS = 32 * NZ
PLANE = ((2, 0), (2, 1), (1, 0), (3, 0), (1, 1), (3, 1), (0, 1))
NBL = 128
CROWS = 136
DECAY = 2.0 / NCHAN


def remote(src, dst, send_sem, recv_sem, device):
    return pltpu.make_async_remote_copy(
        src_ref=src, dst_ref=dst, send_sem=send_sem, recv_sem=recv_sem, device_id=device, device_id_type=MESH
    )


def kernel(
    c_hbm, meas_hbm, rej_hbm, pair_hbm, fetch_hbm, g_hbm, m_hbm, v_hbm,
    go_ref, mo_ref, vo_ref, res_ref,
    c_ref, meas_ref, rej_ref, pair_ref, fetch_ref, g_ref, m_ref, v_ref, in_sem,
    csend, crecv, pick, gsplit, early, grads, state_g, state_m, state_v,
    gpiece, zg, zp, rsn, rsc, rsh, accp, rsp, xs, xr, ressend, resrecv,
    c_ss, c_rs, a1_ss, a1_rs, a2_ss, a2_rs, r1_ss, r1_rs, rc_ss, rc_rs, rh_ss, rh_rs, r2_ss, r2_rs, x_ss, x_rs, o_ss, o_rs,
):
    bl, x = lax.axis_index("bl"), lax.axis_index("ch")
    y, z, c = bl >> 5, (bl >> 1) & (NZ - 1), bl & 1
    s = 2 * y + c
    mates = [2 * ((y + dy) & (NY - 1)) + (c ^ dc) for dy, dc in PLANE]
    plane_at = {dz: 2 * ((z + dz) & (NZ - 1)) for dz in (0, 1, -1, 2, -2, 3, -3, 6, -6)}
    column_of = [32 * ((y + dy) & (NY - 1)) + (c ^ dc) for dy, dc in PLANE] + [32 * y + c]

    def device(k, dz=0, dx=0):
        k = NS - 1 if k is None else k
        return (column_of[k] + plane_at[dz], (x + dx) & (NX - 1) if dx else x)

    toward = jnp.where((z >= 1) & (z <= NZ // 2), 0, 1)

    def device_along(k, direction, planes):
        k = NS - 1 if k is None else k
        return (column_of[k] + 2 * ((z + planes * (2 * direction - 1)) & (NZ - 1)), x)

    barrier = pltpu.get_barrier_semaphore()
    partners = [device(k, j) for j in CENTRES for k in range(NS) if j or k < NS - 1]
    partners += [device(None, n) for n in (2, -2, 1, -1)] + [device(None, 0, dx) for dx in (1, 2, 3)]
    for partner in partners:
        pl.semaphore_signal(barrier, inc=1, device_id=partner, device_id_type=MESH)

    loads = [
        pltpu.make_async_copy(src, dst, in_sem.at[i])
        for i, (src, dst) in enumerate(
            [
                (g_hbm, g_ref), (pair_hbm, pair_ref), (fetch_hbm, fetch_ref), (rej_hbm, rej_ref), (meas_hbm, meas_ref),
                (c_hbm, c_ref), (m_hbm, m_ref), (v_hbm, v_ref),
            ]
        )
    ]
    for load in loads:
        load.start()
    lane8 = lax.broadcasted_iota(I32, (8, 128), 1)
    low8 = lane8 < 64

    def to_pieces(ref, out):
        for t in range(4):
            both = jnp.concatenate([ref[0, :, 128 * t : 128 * t + 128], ref[1, :, 128 * t : 128 * t + 128]], axis=0)
            turned = pltpu.roll(both, 64, 1)
            left = jnp.concatenate([both[0:4], turned[0:4]], axis=0)
            right = jnp.concatenate([turned[4:8], both[4:8]], axis=0)
            out[8 * t : 8 * t + 8, :] = jnp.where(low8, left, right)

    def from_pieces(value, ref):
        for t in range(4):
            both = value[8 * t : 8 * t + 8]
            turned = pltpu.roll(both, 64, 1)
            left = jnp.concatenate([both[0:4], turned[0:4]], axis=0)
            right = jnp.concatenate([turned[4:8], both[4:8]], axis=0)
            mixed = jnp.where(low8, left, right)
            ref[0, :, 128 * t : 128 * t + 128] = mixed[0:4]
            ref[1, :, 128 * t : 128 * t + 128] = mixed[4:8]

    loads[0].wait()
    to_pieces(g_ref, state_g)
    gpiece[0] = state_g[...]

    for load in loads[1:5]:
        load.wait()
    fetch = jnp.where(lax.broadcasted_iota(I32, fetch_ref.shape, 1) == bl, fetch_ref[...], 0).astype(F32)
    fetch = jnp.sum(fetch, axis=1, keepdims=True)
    places = lax.broadcasted_iota(I32, (fetch_ref.shape[0], NBL), 0)
    station = jnp.concatenate(
        [
            jnp.sum(jnp.where(places == pair_ref[i : i + 1, :], fetch, 0.0), axis=0, keepdims=True)
            for i in range(2)
        ],
        axis=0,
    ).astype(I32)
    rel = ((station >> 3) & (NZ - 1)) - z
    rel = jnp.where(rel < 0, rel + NZ, rel)
    slot = jnp.zeros_like(rel)
    for k in range(NZ):
        slot = jnp.where(rel == k, SLOT[k], slot)
    weights = (CELL_READINGS - rej_ref[...]).astype(F32) / CELL_READINGS
    rows = (slot * 32 + (station >> 7) * 8 + (station & 7)).astype(F32)
    loads[5].wait()
    for t in range(4):
        for ri in range(2):
            block = c_ref[ri, :, 128 * t : 128 * t + 128].astype(F32).T
            csend[2 * t, 64 * ri : 64 * ri + 64] = block[0:64]
            csend[2 * t + 1, 64 * ri : 64 * ri + 64] = block[64:128]
    for k in range(NS):
        for ri in range(2):
            csend[k, 128 + 2 * ri : 130 + 2 * ri] = meas_ref[ri, 2 * k : 2 * k + 2, :]
        csend[k, 132:134] = weights[2 * k : 2 * k + 2]
        csend[k, 134:136] = rows

    pl.semaphore_wait(barrier, len(partners))

    def rows_of(device_in_plane):
        return pl.ds(pl.multiple_of(4 * device_in_plane, 4), 4)

    def waiter(ref, send_sem, recv_sem):
        return remote(ref, ref, send_sem, recv_sem, device(0))

    def gains_out(it):
        for pair in ((0, 1), (2, 3), (4,)):
            for k in [*range(NS - 1)] + ([None] if pair[0] < 4 else []):
                to = s if k is None else mates[k]
                for j in pair:
                    remote(
                        gpiece.at[it, rows_of(to)], zg.at[it, BACK[j], rows_of(s)], a1_ss.at[it], a1_rs.at[it, GROUP[j]], device(k, CENTRES[j])
                    ).start()

    def gains_on(it):
        def near_copy(src, width, dst, part, n):
            remote(
                zg.at[it, pl.ds(src, width)], zg.at[it, pl.ds(dst, width)], a2_ss.at[it], a2_rs.at[it, part], device(None, n)
            ).start()

        zg[it, OWN, rows_of(s), :] = gpiece[it, rows_of(s), :]
        waiter(zg.at[it, OWN, pl.ds(0, 28)], a1_ss.at[it], a1_rs.at[it, 3]).wait_recv()
        for i, n in enumerate(STEPS):
            near_copy(OWN, 1, 12 + 3 * i, 1, n)
        waiter(zg.at[it, pl.ds(7, 2)], a1_ss.at[it], a1_rs.at[it, 2]).wait_recv()
        for i, n in enumerate(STEPS):
            near_copy(7, 2, 10 + 3 * i, 1, n)
        for h in range(2):
            waiter(zg.at[it, h], a1_ss.at[it], a1_rs.at[it, h]).wait_recv()
            half = pl.ds(16 * h, 16)
            remote(
                zg.at[it, h, half], zg.at[it, OPPOSITE, half], a2_ss.at[it], a2_rs.at[it, 0], device(None, 2 - 4 * h)
            ).start()
        for i, n in enumerate(STEPS):
            near_copy(0, 2, 2 + 2 * i, 0, n)

    def gains_in(it, part):
        slots = pl.ds(10, 6) if part else pl.ds(2, 5)
        waiter(zg.at[it, slots], a2_ss.at[it], a2_rs.at[it, part]).wait_recv()

    def gains_sent(it):
        waiter(zg.at[it, pl.ds(0, 4)], a1_ss.at[it], a1_rs.at[it, 0]).wait_send()
        waiter(zg.at[it, OWN, pl.ds(0, 28)], a1_ss.at[it], a1_rs.at[it, 0]).wait_send()
        waiter(zg.at[it, pl.ds(0, 11)], a2_ss.at[it], a2_rs.at[it, 0]).wait_send()

    gains_out(0)
    for k in range(NS - 1):
        remote(csend.at[mates[k]], crecv.at[s], c_ss, c_rs.at[s], device(k)).start()
    crecv[s] = csend[s]
    for load in loads[6:]:
        load.wait()
    to_pieces(m_ref, state_m)
    to_pieces(v_ref, state_v)
    gains_on(0)

    sources = [s] + mates[::-1]
    row_id = lax.broadcasted_iota(I32, (ROWS, NBL), 0)

    for i, source in enumerate(sources):
        if i:
            waiter(crecv.at[source], c_ss, c_rs.at[source]).wait_recv()
        for k in range(2):
            row = crecv[source, 134 + k : 135 + k, :].astype(I32)
            pick[:, 256 * i + 128 * k : 256 * i + 128 * k + 128] = jnp.where(row_id == row, 1.0, 0.0).astype(BF16)

    lane32 = lax.broadcasted_iota(I32, (32, 128), 1)
    odd32 = (lane32 & 32) != 0
    odd8 = (lane8 & 32) != 0
    pair32 = lax.broadcasted_iota(I32, (32, 128), 0) >> 2
    chan = 2 * pair32 + jnp.where(odd32, 1, 0)
    a1 = math.exp(-DECAY)

    def decay(steps):
        return jnp.exp(-DECAY * steps.astype(F32))

    whole_chan = chan + 16 * x
    geometric = 1.0 / (1.0 - a1)
    norm = (1.0 - decay(whole_chan + 1)) * geometric + (a1 - decay(NCHAN - whole_chan)) * geometric
    half_norm = BLEND / norm
    from_left = decay(chan + 1)
    from_right = decay(16 - chan)
    near_left = jnp.where(odd32, a1 * a1, a1)
    near_right = jnp.where(odd32, a1, a1 * a1)
    up = jnp.where(odd32, 1.0, a1)
    down = jnp.where(odd32, a1, 1.0)
    to_edge = decay(2 * jnp.where(odd32, pair32, NS - 1 - pair32))
    edge_same = jnp.where(odd32, down, up) * to_edge
    edge_other = jnp.where(odd32, up, down) * to_edge
    take_left, take_right = half_norm * from_left, half_norm * from_right
    weights = []
    for dx in (1, 2, 3):
        source = (x - dx) & (NX - 1)
        gap = jnp.full((8, 128), jnp.abs(x - source), I32)
        is_left = jnp.full((8, 128), x - source, I32) > 0
        used = jnp.where(is_left, jnp.where(odd8, 0, 1), jnp.where(odd8, 1, 0)).astype(F32)
        weights.append((used * decay(16 * (gap - 1)))[0:4])

    def swap(value):
        return jnp.where((lax.broadcasted_iota(I32, value.shape, 1) & 32) != 0, pltpu.roll(value, 32, 1), pltpu.roll(value, 96, 1))

    def smooth(it, total):
        swapped = swap(total)
        edge = total * edge_same + swapped * edge_other
        edge = (edge[0:8] + edge[8:16]) + (edge[16:24] + edge[24:32])
        xs[it] = edge[0:4] + edge[4:8]
        for dx in (2, 1, 3):
            remote(xs.at[it], xr.at[it, dx - 1], x_ss.at[it], x_rs.at[it], device(None, 0, dx)).start()
        right_going = total * up + swapped * down
        left_going = total * down + swapped * up
        zero = jnp.zeros((4, 128), F32)
        lefts, rights = [zero], [zero]
        for k in range(NS - 1):
            lefts.append(a1 * a1 * lefts[-1] + right_going[4 * k : 4 * k + 4])
            q = NS - 1 - k
            rights.append(a1 * a1 * rights[-1] + left_going[4 * q : 4 * q + 4])
        left_all = jnp.concatenate(lefts, axis=0)
        right_all = jnp.concatenate(rights[::-1], axis=0)
        blended = total + a1 * swapped + near_left * left_all + near_right * right_all
        smoothed = (1.0 - BLEND) * total + half_norm * blended
        waiter(xr.at[it], x_ss.at[it], x_rs.at[it]).wait_recv()
        across = xr[it, 0] * weights[0] + xr[it, 1] * weights[1] + xr[it, 2] * weights[2]
        across = jnp.concatenate([across] * 2, axis=0)
        other = swap(across)
        left = jnp.concatenate([jnp.where(odd8, other, across)] * 4, axis=0)
        right = jnp.concatenate([jnp.where(odd8, across, other)] * 4, axis=0)
        return smoothed + take_left * left + take_right * right

    coef = -2.0 / math.sqrt(2.0 * NBL * NS * NZ / (4 * NS * NZ))

    for it in range(ITERS):
        last = it == ITERS - 1
        def split(t):
            block = zg[it, 4 * t : 4 * t + 4].reshape(128, 128).T
            high = block.astype(BF16)
            gsplit[0:128, 128 * t : 128 * t + 128] = high
            gsplit[128:256, 128 * t : 128 * t + 128] = (block - high.astype(F32)).astype(BF16)

        gains_in(it, 1)
        split(2)
        split(3)
        for i in range(NS):
            both = jnp.dot(gsplit[:, 256:512], pick[256:512, 256 * i : 256 * i + 256], preferred_element_type=F32)
            early[i] = both[0:128] + both[128:256]
        gains_in(it, 0)
        split(0)
        split(1)
        for i, source in enumerate(sources):
            both = jnp.dot(gsplit[:, 0:256], pick[0:256, 256 * i : 256 * i + 256], preferred_element_type=F32)
            both = both[0:128] + both[128:256] + early[i]
            ga, gb = both[0:64, 0:128], both[64:128, 0:128]
            gc, gd = both[0:64, 128:256], both[64:128, 128:256]
            cr, ci = crecv[source, 0:64, :], crecv[source, 64:128, :]
            u = ga * gc + gb * gd
            v = gb * gc - ga * gd
            model_re = jnp.sum((u * cr - v * ci).reshape(2, SKY_SOURCES, NBL), axis=1)
            model_im = jnp.sum((u * ci + v * cr).reshape(2, SKY_SOURCES, NBL), axis=1)
            weight = crecv[source, 132:134, :]
            err_re = weight * (crecv[source, 128:130, :] - model_re)
            err_im = weight * (crecv[source, 130:132, :] - model_im)
            if last:
                ressend[source] = jnp.concatenate([err_re, err_im], axis=0)
            wide = (2, SKY_SOURCES, NBL)
            sr = jnp.broadcast_to((coef * err_re)[:, None, :], wide).reshape(64, NBL)
            si = jnp.broadcast_to((coef * err_im)[:, None, :], wide).reshape(64, NBL)
            px = gc * cr + gd * ci
            py = gd * cr - gc * ci
            qx = ga * cr - gb * ci
            qy = ga * ci + gb * cr
            terms = ((sr * px - si * py, sr * py + si * px), (sr * qx + si * qy, sr * qy - si * qx))
            for k in range(2):
                for ri in range(2):
                    value = terms[k][ri]
                    high = value.astype(BF16)
                    where = pl.ds(256 * i + 128 * k, 128)
                    grads[64 * ri : 64 * ri + 64, where] = high
                    grads[128 + 64 * ri : 192 + 64 * ri, where] = (value - high.astype(F32)).astype(BF16)

        def station_sums(begin, end):
            both = lax.dot_general(
                pick[begin:end, :], grads[...], (((1,), (1,)), ((), ())), preferred_element_type=F32
            )
            zp[it, begin:end, :] = both[:, 0:128] + both[:, 128:256]

        station_sums(0, 32 * FIRST)
        for h in range(2):
            remote(
                zp.at[it, pl.ds(32 * OPPOSITE + 16 * h, 16)], rsh.at[it, h], rh_ss.at[it], rh_rs.at[it], device(None, 4 * h - 2)
            ).start()
        for i in (toward, 1 - toward):
            rows = pl.ds(pl.multiple_of(64 + 64 * i, 32), 64)
            remote(zp.at[it, rows], rsn.at[it, i], r1_ss.at[it], r1_rs.at[it], device_along(None, i, 1)).start()
        station_sums(32 * FIRST, ROWS)
        for i in (toward, 1 - toward):
            rows = pl.ds(pl.multiple_of(320 + 96 * i, 32), 96)
            remote(zp.at[it, rows], rsc.at[it, i], rc_ss.at[it], rc_rs.at[it], device_along(None, i, 1)).start()
        if last:
            for k in range(NS - 1):
                remote(ressend.at[mates[k]], resrecv.at[s], o_ss, o_rs, device(k)).start()
            resrecv[s] = ressend[s]
        else:
            waiter(csend.at[pl.ds(0, NS - 1)], c_ss, c_rs.at[s]).wait_send()
        gains_sent(it)
        near = waiter(rsn.at[it], r1_ss.at[it], r1_rs.at[it])
        half = waiter(rsh.at[it], rh_ss.at[it], rh_rs.at[it])
        own = waiter(rsc.at[it], rc_ss.at[it], rc_rs.at[it])
        def far_store(j, acc):
            accp[it, j] = acc

        def far_out(planes):
            first = 0 if planes == 6 else 2
            for side in (toward, 1 - toward):
                j = first + side
                for k in [*range(NS - 1), None]:
                    to = s if k is None else mates[k]
                    remote(
                        accp.at[it, j, rows_of(to)], rsp.at[it, j, rows_of(s)], r2_ss.at[it], r2_rs.at[it, j], device_along(k, side, planes)
                    ).start()

        near.wait_recv()
        half.wait_recv()
        acc = zp[it, 0:64, :] + rsn[it, 0] + rsn[it, 1]
        far_store(0, jnp.concatenate([acc[0:16] + rsh[it, 0], acc[16:32]], axis=0))
        far_store(1, jnp.concatenate([acc[32:48], acc[48:64] + rsh[it, 1]], axis=0))
        far_out(6)
        own.wait_recv()
        acc = zp[it, 32 * FIRST : 32 * FIRST + 96, :] + rsc[it, 0] + rsc[it, 1]
        for j in (2, 3, 4):
            far_store(j, acc[32 * j - 64 : 32 * j - 32])
        far_out(3)
        for k in range(NS - 1):
            remote(
                accp.at[it, NC - 1, rows_of(mates[k])], rsp.at[it, NC - 1, rows_of(s)], r2_ss.at[it], r2_rs.at[it, NC - 1], device(k)
            ).start()
        rsp[it, NC - 1, rows_of(s), :] = accp[it, NC - 1, rows_of(s), :]
        near.wait_send()
        half.wait_send()
        own.wait_send()
        if last:
            result = waiter(resrecv.at[pl.ds(0, NS - 1)], o_ss, o_rs)
            result.wait_send()
            result.wait_recv()
            for k in range(NS):
                for ri in range(2):
                    res_ref[ri, 2 * k : 2 * k + 2, :] = resrecv[k, 2 * ri : 2 * ri + 2, :]
        waiter(rsp.at[it, NC - 1, pl.ds(0, 28)], r2_ss.at[it], r2_rs.at[it, NC - 1]).wait_recv()
        for j in (2, 3):
            waiter(rsp.at[it, j], r2_ss.at[it], r2_rs.at[it, j]).wait_recv()
        total = rsp[it, 4] + rsp[it, 2] + rsp[it, 3]
        for j in (0, 1):
            waiter(rsp.at[it, j], r2_ss.at[it], r2_rs.at[it, j]).wait_recv()
        total = total + rsp[it, 0] + rsp[it, 1]
        smoothed = smooth(it, total)
        tally = STEP + it + 1
        new_m = BETA_ONE * state_m[...] + (1.0 - BETA_ONE) * smoothed
        new_v = BETA_TWO * state_v[...] + (1.0 - BETA_TWO) * smoothed * smoothed
        rate = LEARN_RATE / (1.0 - BETA_ONE**tally)
        new_g = state_g[...] - rate * new_m / (jnp.sqrt(new_v * (1.0 / (1.0 - BETA_TWO**tally))) + ADAM_EPSILON)
        if last:
            from_pieces(new_g, go_ref)
            from_pieces(new_m, mo_ref)
            from_pieces(new_v, vo_ref)
        else:
            gpiece[it + 1] = new_g
            gains_out(it + 1)
            state_g[...] = new_g
            state_m[...] = new_m
            state_v[...] = new_v
        waiter(rsp.at[it, pl.ds(0, NC - 1)], r2_ss.at[it], r2_rs.at[it, 0]).wait_send()
        waiter(rsp.at[it, NC - 1, pl.ds(0, 28)], r2_ss.at[it], r2_rs.at[it, 2]).wait_send()
        waiter(xr.at[it], x_ss.at[it], x_rs.at[it]).wait_send()
        if not last:
            gains_on(it + 1)


def store(*refs):
    sem = refs[-1]
    copies = [pltpu.make_async_copy(refs[i], refs[4 + i], sem.at[i]) for i in range(4)]
    for copy in copies:
        copy.start()
    for copy in copies:
        copy.wait()


def on_device(coherency, measured, rejected, pairs, fetch_lists, gains, first, second):
    args = (
        coherency, jnp.swapaxes(measured, 1, 2), rejected.T, pairs.T, fetch_lists.T, gains, first, second,
    )
    args = [pltpu.with_memory_space_constraint(a, pltpu.HBM) for a in args]
    out = [jax.ShapeDtypeStruct(gains.shape, F32)] * 3 + [jax.ShapeDtypeStruct(args[1].shape, F32)]
    vmem = pl.BlockSpec(memory_space=pltpu.VMEM)
    anywhere = pl.BlockSpec(memory_space=pl.ANY)
    hbm = pl.BlockSpec(memory_space=pltpu.HBM)
    sem = pltpu.SemaphoreType.DMA
    buf = pltpu.VMEM
    results = pl.pallas_call(
        kernel,
        out_shape=out,
        in_specs=[hbm] * 8,
        out_specs=[vmem] * 4,
        scratch_shapes=[
            *[buf(a.shape, a.dtype) for a in args],
            sem((8,)),
            buf((NS, CROWS, NBL), F32),
            buf((NS, CROWS, NBL), F32),
            buf((ROWS, 2 * NBL * NS), BF16),
            buf((256, ROWS), BF16),
            buf((NS, 128, 256), F32),
            buf((256, 2 * NBL * NS), BF16),
            buf((32, 128), F32),
            buf((32, 128), F32),
            buf((32, 128), F32),
            buf((ITERS, 32, 128), F32),
            buf((ITERS, NZ, 32, 128), F32),
            buf((ITERS, ROWS, 128), F32),
            buf((ITERS, 2, 64, 128), F32),
            buf((ITERS, 2, 96, 128), F32),
            buf((ITERS, 2, 16, 128), F32),
            buf((ITERS, NC, 32, 128), F32),
            buf((ITERS, NC, 32, 128), F32),
            buf((ITERS, 4, 128), F32),
            buf((ITERS, 3, 4, 128), F32),
            buf((NS, 4, 128), F32),
            buf((NS, 4, 128), F32),
            sem, sem((NS,)),
            sem((ITERS,)), sem((ITERS, 4)),
            sem((ITERS,)), sem((ITERS, 2)),
            sem((ITERS,)), sem((ITERS,)),
            sem((ITERS,)), sem((ITERS,)),
            sem((ITERS,)), sem((ITERS,)),
            sem((ITERS,)), sem((ITERS, NC)),
            sem((ITERS,)), sem((ITERS,)),
            sem, sem,
        ],
        compiler_params=pltpu.CompilerParams(collective_id=0, has_side_effects=True, vmem_limit_bytes=32 * 2**20),
        cost_estimate=pl.CostEstimate(flops=4 * 10**9, bytes_accessed=2**20, transcendentals=10**4),
        name="calibrate",
    )(*args)
    new_g, new_m, new_v, residual = pl.pallas_call(
        store, out_shape=out, in_specs=[anywhere] * 4, out_specs=[hbm] * 4, scratch_shapes=[sem((4,))], name="store",
        compiler_params=pltpu.CompilerParams(vmem_limit_bytes=32 * 2**20),
    )(*results)
    return new_g, new_m, new_v, jnp.swapaxes(residual, 1, 2)


def solution(mesh):
    split = P(None, "bl", "ch")
    return jax.shard_map(
        on_device,
        mesh=mesh,
        in_specs=(split, split, P("bl", "ch"), P("bl", None), P(), split, split, split),
        out_specs=(split,) * 4,
        check_vma=False,
    )
```
